256 devices in a mesh: gx: 8 (over x, core), gy: 4 (over y), al: 8 (over z).
Axes of the slice: x: 4, y: 4, z: 8, core: 2. Of those that a mesh axis runs over, the one named last changes fastest.
Arguments:
- volt_now: float32 [16, 512, 2048], P('al', 'gx', 'gy'), may hold values from -8 to 8
- volt_prev: float32 [16, 512, 2048], P('al', 'gx', 'gy'), may hold values from -8 to 8
- cap_term: float32 [16, 512, 2048], P('al', 'gx', 'gy'), may hold values from 0.05 to 0.5
- edge_x: float32 [16, 512, 2048], P('al', 'gx', 'gy'), may hold values from 0.2 to 5
- edge_y: float32 [16, 512, 2048], P('al', 'gx', 'gy'), may hold values from 0.2 to 5
- via_below: float32 [16, 512, 2048], P('al', 'gx', 'gy'), may hold values from 0.5 to 8
- cell_ids: int32 [512, 2048], P('gx', 'gy'), may hold values from 0 to 63
- placed: int32 [512, 2048], P('gx', 'gy'), may hold values 0 or 1
- current_table: float32 [64], replicated, may hold values from 0.5 to 4
Outputs:
- solution_field: float32 [16, 512, 2048], P('al', 'gx', 'gy')
- residual: float32 [16, 512, 2048], P('al', 'gx', 'gy')
The draws below stay inside these ranges and needn't reach their ends.
All inputs are finite; a program needn't handle non-finite values. No bound on the sum of `placed` on one device may be relied on, other than what follows from the above.
Results may differ from the reference program's by a relative error of at most 0.0059.
Values sent between devices are 32-bit elements; how exact they have to be, the bound alone decides.
A program may use at most 64 MiB of HBM per device.

```python
import math
import jax
import jax.numpy as jnp
import numpy as np
from jax import lax

NTYPES = 64
ITERS = 8
NL = 16
NX = 512
NY = 2048


def with_ends(array, own_key, low, largest):
    place = [jax.random.randint(jax.random.fold_in(own_key, axis), (), 0, length) for axis, length in enumerate(array.shape)]
    longest = array.shape.index(max(array.shape))
    next_to = place[:longest] + [(place[longest] + 1) % array.shape[longest]] + place[longest + 1:]
    return array.at[tuple(place)].set(low).at[tuple(next_to)].set(largest)


def levels(stream_key, shape, split, smallest, largest):
    level = 1.0
    for axis_at, parts in split:
        draws = jax.random.uniform(jax.random.fold_in(jax.random.fold_in(stream_key, 6), axis_at), (parts,), jnp.float32, smallest / len(split), largest / len(split))
        level = level * jnp.repeat(jnp.exp(draws), shape[axis_at] // parts).reshape((-1,) + (1,) * (len(shape) - 1 - axis_at))
    return level


def rank_table(number_of, lean):
    weights = [(1 << 20) // math.isqrt(standing ** lean) + 1 for standing in range(1, number_of + 1)]
    width = 1 + sum(weights) // (1 << 30)
    return np.cumsum(np.array([max(1, weight // width) for weight in weights]))


def ranked_ids(rng, shape, count, lean):
    listing = rank_table(count, lean)
    ticket = jax.random.randint(jax.random.fold_in(rng, 1), shape, 0, int(listing[count - 1]))
    grade = jnp.searchsorted(jnp.asarray(listing, jnp.int32), ticket, side="right")
    return jax.random.permutation(jax.random.fold_in(rng, 2), count)[grade].astype(jnp.int32)


def normal_values(rng, shape, spread, most, cuts=(), held_as=jnp.bfloat16):
    result = spread * jax.random.normal(rng, shape, jnp.float32)
    if cuts:
        result = result * levels(rng, shape, cuts, -0.22, 0.18)
    return jnp.clip(result, -most, most).astype(held_as)


def setup_inputs(seed: int = 0) -> dict:
    arg_keys = jax.random.split(jax.random.key(seed), 10)
    return {
        "volt_now": normal_values(arg_keys[0], (NL, NX, NY), 2.0, 8.0, ((0, 8), (1, 8), (2, 4)), jnp.float32),
        "volt_prev": normal_values(arg_keys[1], (NL, NX, NY), 2.0, 8.0, ((0, 8), (1, 8), (2, 4)), jnp.float32),
        "cap_term": jnp.clip(jnp.exp(math.log(0.5) - 2.3025851 * jax.random.uniform(arg_keys[2], (NL, NX, NY), jnp.float32) ** levels(arg_keys[2], (NL, NX, NY), ((0, 8), (1, 8), (2, 4)), -0.2, 0.2)), 0.05, 0.5),
        "edge_x": jnp.clip(jnp.exp(math.log(5.0) - 3.218876 * jax.random.uniform(arg_keys[3], (NL, NX, NY), jnp.float32) ** levels(arg_keys[3], (NL, NX, NY), ((0, 8), (1, 8), (2, 4)), -0.2, 0.2)), 0.2, 5.0),
        "edge_y": jnp.clip(jnp.exp(math.log(5.0) - 3.218876 * jax.random.uniform(arg_keys[4], (NL, NX, NY), jnp.float32) ** levels(arg_keys[4], (NL, NX, NY), ((0, 8), (1, 8), (2, 4)), -0.2, 0.2)), 0.2, 5.0),
        "via_below": jnp.clip(jnp.exp(math.log(8.0) - 2.7725887 * jax.random.uniform(arg_keys[5], (NL, NX, NY), jnp.float32) ** levels(arg_keys[5], (NL, NX, NY), ((0, 8), (1, 8), (2, 4)), -0.2, 0.2)), 0.5, 8.0),
        "cell_ids": with_ends(ranked_ids(arg_keys[6], (NX, NY), NTYPES, 2), jax.random.fold_in(arg_keys[6], 3), 0, NTYPES - 1).astype(jnp.int32),
        "placed": with_ends((jax.random.randint(arg_keys[7], (NX, NY), 0, 4) < 3).astype(jnp.int32), jax.random.fold_in(arg_keys[7], 1), 0, 1),
        "current_table": jnp.clip(jnp.exp(jax.random.uniform(arg_keys[8], (NTYPES,), jnp.float32, math.log(0.5), math.log(4.0))), 0.5, 4.0),
    }


def prepare(cap_term, edge_x, edge_y, via_below):
    shape = edge_x.shape
    li = lax.broadcasted_iota(jnp.int32, shape, 0)
    xi = lax.broadcasted_iota(jnp.int32, shape, 1)
    yi = lax.broadcasted_iota(jnp.int32, shape, 2)
    ex = jnp.where(xi < shape[1] - 1, edge_x, 0.0)
    ey = jnp.where(yi < shape[2] - 1, edge_y, 0.0)
    vb = jnp.where(li > 0, via_below, 0.0)
    exl = jnp.pad(ex, ((0, 0), (1, 0), (0, 0)))[:, :-1, :]
    eyl = jnp.pad(ey, ((0, 0), (0, 0), (1, 0)))[:, :, :-1]
    via_below_admittance = jnp.pad(vb, ((0, 1), (0, 0), (0, 0)))[1:, :, :]
    diag = cap_term + ex + exl + ey + eyl + vb + via_below_admittance
    return ex, ey, vb, exl, eyl, via_below_admittance, diag


def operate(v, ex, ey, vb, exl, eyl, via_below_admittance, diag):
    padded = jnp.pad(v, 1)
    side = ex * padded[1:-1, 2:, 1:-1] + exl * padded[1:-1, :-2, 1:-1]
    side = side + ey * padded[1:-1, 1:-1, 2:] + eyl * padded[1:-1, 1:-1, :-2]
    side = side + via_below_admittance * padded[2:, 1:-1, 1:-1] + vb * padded[:-2, 1:-1, 1:-1]
    return diag * v - side


def pivots(diag, vb):
    rows = [diag[0]]
    for layer_position in range(1, diag.shape[0]):
        rows.append(diag[layer_position] - vb[layer_position] * vb[layer_position] / rows[-1])
    return rows


def precond(r, work_vector, vb, via_below_admittance):
    count = r.shape[0]
    eliminated_factor = []
    preceding_entry = jnp.zeros_like(r[0])
    for layer_position in range(count):
        preceding_entry = (r[layer_position] + vb[layer_position] * preceding_entry) / work_vector[layer_position]
        eliminated_factor.append(preceding_entry)
    out = [None] * count
    following_entry = jnp.zeros_like(r[0])
    for layer_position in range(count - 1, -1, -1):
        following_entry = eliminated_factor[layer_position] + (via_below_admittance[layer_position] / work_vector[layer_position]) * following_entry
        out[layer_position] = following_entry
    return jnp.stack(out)


def reference(volt_now, volt_prev, cap_term, edge_x, edge_y, via_below, cell_ids, placed, current_table):
    ex, ey, vb, exl, eyl, via_below_admittance, diag = prepare(cap_term, edge_x, edge_y, via_below)
    types = lax.broadcasted_iota(jnp.int32, (current_table.shape[0],) + cell_ids.shape, 0)
    chosen = jnp.sum(jnp.where(cell_ids[None] == types, current_table[:, None, None], 0.0), axis=0)
    current = chosen * placed.astype(jnp.float32)
    li = lax.broadcasted_iota(jnp.int32, volt_now.shape, 0)
    stamp = jnp.where(li == 0, current[None], 0.0)
    rhs = cap_term * (4.0 * volt_now - volt_prev) / 3.0 + stamp
    work_vector = pivots(diag, vb)
    solution_field = jnp.zeros_like(rhs)
    residual = rhs
    zvec = precond(residual, work_vector, vb, via_below_admittance)
    rho = jnp.sum(residual * zvec)
    direction = zvec
    for step in range(ITERS):
        image = operate(direction, ex, ey, vb, exl, eyl, via_below_admittance, diag)
        alpha = rho / jnp.sum(direction * image)
        solution_field = solution_field + alpha * direction
        residual = residual - alpha * image
        if step + 1 < ITERS:
            zvec = precond(residual, work_vector, vb, via_below_admittance)
            rho_new = jnp.sum(residual * zvec)
            direction = zvec + (rho_new / rho) * direction
            rho = rho_new
    return solution_field, residual
```

```python
import functools

import jax
import jax.numpy as jnp
from jax import lax
from jax.experimental import pallas as pl
from jax.experimental.pallas import tpu as pltpu
from jax.sharding import PartitionSpec as P

ITERS = 8
MESH = pl.DeviceIdType.MESH
EX, EY, VB, WI, UP, DN, EXL, EYL = range(8)
RHS = 4
GHOST = 8
TILE = 8
LANES = 128


def rows_at(tile):
    return pl.ds(pl.multiple_of(tile * TILE, TILE), TILE)


def kernel(
    axes, table, vn, vp, cap, ex, ey, vb, ids, placed, xo, ro,
    pack, recv, coef, s_buf, u_buf, ysend, yrecv, cur, part, gath, packo, recvo,
    t_ss, t_rs, l_s, x_ss, x_rs, y_ss, y_rs, r_ss, r_rs, o_ss, o_rs, lo_s,
):
    n_gx, n_gy, n_al = axes
    gx, gy, al = lax.axis_index("gx"), lax.axis_index("gy"), lax.axis_index("al")
    group, cols, rows = vn.shape
    layers = group * n_al
    width = rows // n_al
    half = cols // 2
    half_tiles = half // TILE
    own_tiles = cols // TILE
    tiles = own_tiles + 2
    odd = gy % 2
    strip = al * (1 - odd) + (n_al - 1 - al) * odd
    turn = 1 - 2 * odd

    def home(j):
        return j * (1 - odd) + (n_al - 1 - j) * odd

    at_hi = strip // (n_al - 1)
    at_lo = (n_al - 1 - strip) // (n_al - 1)
    right = {"gy": (gy + at_hi) % n_gy, "al": al + turn * (1 - at_hi)}
    left = {"gy": (gy + (n_gy - 1) * at_lo) % n_gy, "al": al - turn * (1 - at_lo)}
    fore = {"gx": (gx + 1) % n_gx}
    back = {"gx": (gx + n_gx - 1) % n_gx}
    al_peers = [{"al": (al + k) % n_al} for k in range(1, n_al)]
    gx_peers = [{"gx": (gx + k) % n_gx} for k in range(1, n_gx)]
    gy_peers = [{"gy": (gy + k) % n_gy} for k in range(1, n_gy)]
    sum_groups = (gx_peers, gy_peers, al_peers)

    barrier = pltpu.get_barrier_semaphore()
    for peer in al_peers + gx_peers + gy_peers:
        pl.semaphore_signal(barrier, inc=1, device_id=peer, device_id_type=MESH)
    pl.semaphore_wait(barrier, len(al_peers + gx_peers + gy_peers))

    lane = lax.broadcasted_iota(jnp.int32, (TILE, LANES), 1)
    sub = lax.broadcasted_iota(jnp.int32, (TILE, LANES), 0)
    low = lane < width
    zero = jnp.zeros((TILE, LANES), jnp.float32)

    def value(which, layer, tile, q):
        at = (layer, rows_at(tile), pl.ds(q * LANES, LANES))
        if which == EX:
            last = (gx * cols + tile * TILE + sub) == n_gx * cols - 1
            return jnp.where(last, 0.0, ex[at])
        if which == EY:
            last = (gy * rows + q * LANES + lane) == n_gy * rows - 1
            return jnp.where(last, 0.0, ey[at])
        if which == VB:
            return jnp.where(al * group + layer == 0, 0.0, vb[at])
        if which == WI:
            return cap[at]
        return cap[at] * (4.0 * vn[at] - vp[at]) / 3.0

    def pack_array(which):
        for layer in range(group):
            def one(tile, c):
                for q in range(rows // LANES):
                    lo = value(which, layer, tile, q)
                    hi = value(which, layer, tile + half_tiles, q)
                    pack[which, 2 * q, layer, rows_at(tile)] = jnp.where(low, lo, pltpu.roll(hi, width, 1))
                    pack[which, 2 * q + 1, layer, rows_at(tile)] = jnp.where(low, pltpu.roll(lo, width, 1), hi)
                return c

            lax.fori_loop(0, half_tiles, one, 0)

    def own_copy(which):
        return pltpu.make_async_copy(
            pack.at[which, strip], recv.at[which, pl.ds(group * al, group)], l_s.at[which]
        )

    for which in range(5):
        pack_array(which)
        for k in (4, 3, 5, 2, 6, 1, 7):
            to = (al + k) % n_al
            pltpu.make_async_remote_copy(
                src_ref=pack.at[which, home(to)],
                dst_ref=recv.at[which, pl.ds(group * al, group)],
                send_sem=t_ss.at[which],
                recv_sem=t_rs.at[which],
                device_id={"al": to},
                device_id_type=MESH,
            ).start()
        own_copy(which).start()

    def wait_array(which):
        many = recv.at[which, pl.ds(0, group * (n_al - 1))]
        pltpu.make_async_remote_copy(
            many, many, t_ss.at[which], t_rs.at[which], device_id={"al": al_peers[0]["al"]}, device_id_type=MESH
        ).wait_recv()
        own_copy(which).wait()

    mine = ids.at[:, pl.ds(pl.multiple_of((strip // 2) * LANES, LANES), LANES)]
    mine_placed = placed.at[:, pl.ds(pl.multiple_of((strip // 2) * LANES, LANES), LANES)]

    def stamp(tile, c):
        code = mine[rows_at(tile)]
        total = zero
        for kind in range(table.shape[0]):
            total = jnp.where(code == kind, table[kind], total)
        total = total * mine_placed[rows_at(tile)].astype(jnp.float32)
        total = jnp.where(strip % 2 == 0, total, pltpu.roll(total, width, 1))
        cur[rows_at(tile)] = total
        return c

    lax.fori_loop(0, own_tiles, stamp, 0)

    def unpack(which, dest):
        def one(layer, c):
            for tile in range(half_tiles):
                v = recv[which, layer, rows_at(tile)]
                dest[layer, rows_at(tile + 1)] = jnp.where(low, v, 0.0)
                dest[layer, rows_at(tile + 1 + half_tiles)] = jnp.where(low, pltpu.roll(v, width, 1), 0.0)
            return c

        lax.fori_loop(0, layers, one, 0)

    def x_copies(which, dest):
        down = pltpu.make_async_remote_copy(
            dest.at[:, pl.ds(cols, GHOST)], dest.at[:, pl.ds(0, GHOST)],
            x_ss.at[which, 0], x_rs.at[which, 0], device_id=fore, device_id_type=MESH,
        )
        up = pltpu.make_async_remote_copy(
            dest.at[:, pl.ds(GHOST, GHOST)], dest.at[:, pl.ds(GHOST + cols, GHOST)],
            x_ss.at[which, 1], x_rs.at[which, 1], device_id=back, device_id_type=MESH,
        )
        return down, up

    def y_copies(which):
        out = []
        for way, peer in ((0, right), (1, left)):
            out.append(
                pltpu.make_async_remote_copy(
                    ysend.at[which, way], yrecv.at[which, way],
                    y_ss.at[which, way], y_rs.at[which, way], device_id=peer, device_id_type=MESH,
                )
            )
        return out

    def start_x(which, dest):
        for copy in x_copies(which, dest):
            copy.start()

    def start_y(which, dest):
        for copy in x_copies(which, dest):
            copy.wait()

        def trim(layer, c):
            dest[layer, rows_at(0)] = jnp.where(gx == 0, 0.0, dest[layer, rows_at(0)])
            dest[layer, rows_at(tiles - 1)] = jnp.where(gx == n_gx - 1, 0.0, dest[layer, rows_at(tiles - 1)])
            return c

        lax.fori_loop(0, layers, trim, 0)

        def one(tile, c):
            to_right, to_left = zero, zero
            for layer in range(layers):
                here = lane // GHOST == layer
                v = dest[layer, rows_at(tile)]
                to_right = jnp.where(here, pltpu.roll(v, (GHOST * layer - (width - GHOST)) % LANES, 1), to_right)
                to_left = jnp.where(here, pltpu.roll(v, GHOST * layer, 1), to_left)
            ysend[which, 0, rows_at(tile)] = to_right
            ysend[which, 1, rows_at(tile)] = to_left
            return c

        lax.fori_loop(0, tiles, one, 0)
        for copy in y_copies(which):
            copy.start()

    first = gy * n_al + strip == 0
    final = gy * n_al + strip == n_gy * n_al - 1

    def finish_y(which, dest):
        for copy in y_copies(which):
            copy.wait()

        def one(tile, c):
            from_left = jnp.where(first, 0.0, yrecv[which, 0, rows_at(tile)])
            from_right = jnp.where(final, 0.0, yrecv[which, 1, rows_at(tile)])
            for layer in range(layers):
                v = dest[layer, rows_at(tile)]
                lft = pltpu.roll(from_left, (LANES - GHOST - GHOST * layer) % LANES, 1)
                rgt = pltpu.roll(from_right, (width - GHOST * layer) % LANES, 1)
                edge = jnp.where(lane < width + GHOST, rgt, jnp.where(lane >= LANES - GHOST, lft, 0.0))
                dest[layer, rows_at(tile)] = jnp.where(low, v, edge)
            return c

        lax.fori_loop(0, tiles, one, 0)

    def before(v, previous):
        return pltpu.roll(jnp.where(sub == TILE - 1, previous, v), 1, 0)

    def after(v, following):
        return pltpu.roll(jnp.where(sub == 0, following, v), TILE - 1, 0)

    u0 = u_buf.at[0]
    c_of = [coef.at[i] for i in range(8)]

    wait_array(EX)
    unpack(EX, c_of[EX])
    start_x(EX, c_of[EX])
    wait_array(EY)
    unpack(EY, c_of[EY])
    start_x(EY, c_of[EY])
    start_y(EX, c_of[EX])
    wait_array(VB)
    unpack(VB, c_of[VB])
    start_x(VB, c_of[VB])
    start_y(EY, c_of[EY])
    finish_y(EX, c_of[EX])
    start_y(VB, c_of[VB])
    finish_y(EY, c_of[EY])

    def lefts(tile, c):
        above = jnp.maximum(tile - 1, 0)
        for layer in range(layers):
            coef[EXL, layer, rows_at(tile)] = before(coef[EX, layer, rows_at(tile)], coef[EX, layer, rows_at(above)])
            coef[EYL, layer, rows_at(tile)] = pltpu.roll(coef[EY, layer, rows_at(tile)], 1, 1)
        return c

    lax.fori_loop(0, tiles, lefts, 0)
    finish_y(VB, c_of[VB])
    wait_array(WI)

    def pivots(tile, c):
        at = rows_at(tile + 1)
        upper = tile // half_tiles
        inverse = zero
        for layer in range(layers):
            held = recv[WI, layer, rows_at(tile % half_tiles)]
            held = jnp.where(upper == 0, held, pltpu.roll(held, width, 1))
            below = coef[VB, layer, at]
            diag = held + coef[EX, layer, at] + coef[EXL, layer, at] + coef[EY, layer, at] + coef[EYL, layer, at] + below
            if layer + 1 < layers:
                diag = diag + coef[VB, layer + 1, at]
            if layer:
                diag = diag - below * below * inverse
            inverse = jnp.where(low, 1.0 / diag, 0.0)
            coef[WI, layer, at] = inverse
        return c

    lax.fori_loop(0, own_tiles, pivots, 0)
    start_x(WI, c_of[WI])
    start_y(WI, c_of[WI])
    wait_array(RHS)
    unpack(RHS, u0)

    def add_stamp(tile, c):
        u0[0, rows_at(tile + 1)] = u0[0, rows_at(tile + 1)] + jnp.where(low, cur[rows_at(tile)], 0.0)
        return c

    lax.fori_loop(0, own_tiles, add_stamp, 0)
    start_x(RHS, u0)
    finish_y(WI, c_of[WI])

    def factors(tile, c):
        at = rows_at(tile)
        for layer in range(layers):
            inverse = coef[WI, layer, at]
            coef[UP, layer, at] = coef[VB, layer, at] * inverse
            if layer + 1 < layers:
                coef[DN, layer, at] = coef[VB, layer + 1, at] * inverse
        return c

    lax.fori_loop(0, tiles, factors, 0)
    start_y(RHS, u0)
    finish_y(RHS, u0)

    def solve(us, at):
        kept = []
        d = None
        for layer in range(layers):
            term = us[layer] * coef[WI, layer, at]
            d = term if layer == 0 else term + coef[UP, layer, at] * d
            kept.append(d)
        for layer in range(layers - 2, -1, -1):
            kept[layer] = kept[layer] + coef[DN, layer, at] * kept[layer + 1]
        return kept

    def is_own(tile):
        return jnp.logical_and(tile >= 1, tile <= own_tiles)

    def begin(tile, acc):
        at = rows_at(tile)
        us = [u_buf[0, layer, at] for layer in range(layers)]
        ss = solve(us, at)
        total = zero
        for layer in range(layers):
            s_buf[0, layer, at] = ss[layer]
            total = total + ss[layer] * us[layer]
        return acc + jnp.where(is_own(tile), total, 0.0)

    part[0] = lax.fori_loop(0, tiles, begin, zero)

    def apply(k, onward):
        twice = jnp.where(k == 0, 1.0, 2.0)
        once = jnp.where(k == 0, 0.0, 1.0)
        older = jnp.maximum(k - 1, 0)

        def one(tile, accs):
            at = rows_at(tile)
            above = rows_at(jnp.maximum(tile - 1, 0))
            under = rows_at(jnp.minimum(tile + 1, tiles - 1))
            cross, square = zero, zero
            us = []
            for layer in range(layers):
                v = s_buf[k, layer, at]
                t = coef[EX, layer, at] * after(v, s_buf[k, layer, under])
                t = t + coef[EXL, layer, at] * before(v, s_buf[k, layer, above])
                t = t + coef[EY, layer, at] * pltpu.roll(v, LANES - 1, 1)
                t = t + coef[EYL, layer, at] * pltpu.roll(v, 1, 1)
                u = twice * t - once * u_buf[older, layer, at]
                u_buf[k + 1, layer, at] = u
                cross = cross + v * u
                us.append(u)
            if onward:
                ss = solve(us, at)
                for layer in range(layers):
                    s_buf[k + 1, layer, at] = ss[layer]
                    square = square + ss[layer] * us[layer]
            own = is_own(tile)
            return accs[0] + jnp.where(own, cross, 0.0), accs[1] + jnp.where(own, square, 0.0)

        cross, square = lax.fori_loop(0 if onward else 1, tiles if onward else tiles - 1, one, (zero, zero))
        part[2 * k + 1] = cross
        if onward:
            part[2 * k + 2] = square

    def steps(k, c):
        apply(k, True)
        return c

    lax.fori_loop(0, ITERS - 1, steps, 0)
    apply(ITERS - 1, False)

    n_sums = 2 * ITERS
    gath[0, 0] = jnp.sum(jnp.where(low[None], part[...], 0.0), axis=1)
    for stage, peers in enumerate(sum_groups):
        for slot, peer in enumerate(peers):
            pltpu.make_async_remote_copy(
                gath.at[stage, 0], gath.at[stage, slot + 1], r_ss.at[stage], r_rs.at[stage],
                device_id=peer, device_id_type=MESH,
            ).start()
        many = gath.at[stage, pl.ds(1, len(peers))]
        pltpu.make_async_remote_copy(
            many, many, r_ss.at[stage], r_rs.at[stage], device_id=peers[0], device_id_type=MESH
        ).wait()
        gath[stage + 1, 0] = jnp.sum(gath[stage, 0 : len(peers) + 1], axis=0)
    sums = jnp.broadcast_to(jnp.sum(gath[len(sum_groups), 0], axis=1, keepdims=True), (n_sums, LANES))
    pair = [sums[i : i + 1] for i in range(n_sums)]
    moment = [pair[0], pair[1]]
    for i in range(2, n_sums):
        moment.append(2.0 * pair[i] - pair[i % 2])
    q = [moment[0] - moment[1]]
    for i in range(1, n_sums - 1):
        q.append(moment[i] - 0.5 * (moment[i + 1] + moment[i - 1]))
    mat = [[0.5 * (q[i + j] + q[abs(i - j)]) for j in range(ITERS)] for i in range(ITERS)]
    vec = [moment[i] for i in range(ITERS)]
    inv = []
    for k in range(ITERS):
        inv.append(1.0 / mat[k][k])
        for i in range(k + 1, ITERS):
            ratio = mat[k][i] * inv[k]
            for j in range(i, ITERS):
                mat[i][j] = mat[i][j] - ratio * mat[k][j]
            vec[i] = vec[i] - ratio * vec[k]
    c = [None] * ITERS
    for k in range(ITERS - 1, -1, -1):
        total = vec[k]
        for j in range(k + 1, ITERS):
            total = total - mat[k][j] * c[j]
        c[k] = total * inv[k]
    e = []
    for n in range(ITERS + 1):
        total = jnp.ones_like(c[0]) if n == 0 else jnp.zeros_like(c[0])
        if n < ITERS:
            total = total - c[n]
        if n >= 1:
            total = total + (1.0 if n == 1 else 0.5) * c[n - 1]
        if n + 1 < ITERS:
            total = total + 0.5 * c[n + 1]
        e.append(total)
    cs = [jnp.broadcast_to(a, (TILE, LANES)) for a in c]
    es = [jnp.broadcast_to(a, (TILE, LANES)) for a in e]

    def out_copy(which, to):
        return pltpu.make_async_remote_copy(
            packo.at[which, to], recvo.at[which, strip], o_ss.at[which], o_rs.at[which],
            device_id={"al": to}, device_id_type=MESH,
        )

    def combine(buf, weights, layer, tile):
        at = rows_at(tile)
        total = weights[0] * buf[0, layer, at]
        for j in range(1, len(weights)):
            total = total + weights[j] * buf[j, layer, at]
        return total

    for k in (4, 3, 5, 2, 6, 1, 7, 0):
        to = (al + k) % n_al
        for which, buf, weights in ((0, s_buf, cs), (1, u_buf, es)):
            for member in range(group):
                layer = to * group + member

                def one(tile, carry):
                    lo = combine(buf, weights, layer, tile + 1)
                    hi = combine(buf, weights, layer, tile + 1 + half_tiles)
                    packo[which, to, member, rows_at(tile)] = jnp.where(low, lo, pltpu.roll(hi, width, 1))
                    return carry

                lax.fori_loop(0, half_tiles, one, 0)
            if k:
                out_copy(which, to).start()
            else:
                pltpu.make_async_copy(packo.at[which, al], recvo.at[which, strip], lo_s.at[which]).start()

    for which, dest in ((0, xo), (1, ro)):
        many = recvo.at[which, pl.ds(0, n_al - 1)]
        pltpu.make_async_remote_copy(
            many, many, o_ss.at[which], o_rs.at[which], device_id=al_peers[0], device_id_type=MESH
        ).wait()
        pltpu.make_async_copy(packo.at[which, al], recvo.at[which, strip], lo_s.at[which]).wait()

        def one(tile, carry):
            for member in range(group):
                for tq in range(rows // LANES):
                    p = recvo[which, 2 * tq, member, rows_at(tile)]
                    r = recvo[which, 2 * tq + 1, member, rows_at(tile)]
                    dest[member, rows_at(tile), pl.ds(tq * LANES, LANES)] = jnp.where(low, p, pltpu.roll(r, width, 1))
                    dest[member, rows_at(tile + half_tiles), pl.ds(tq * LANES, LANES)] = jnp.where(
                        low, pltpu.roll(p, width, 1), r
                    )
            return carry

        lax.fori_loop(0, half_tiles, one, 0)

    for which in range(5):
        many = recv.at[which, pl.ds(0, group * (n_al - 1))]
        pltpu.make_async_remote_copy(
            many, many, t_ss.at[which], t_rs.at[which], device_id=al_peers[0], device_id_type=MESH
        ).wait_send()


def solution(mesh):
    axes = (mesh.shape["gx"], mesh.shape["gy"], mesh.shape["al"])

    def block(volt_now, volt_prev, cap_term, edge_x, edge_y, via_below, cell_ids, placed, current_table):
        group, cols, rows = volt_now.shape
        layers = group * axes[2]
        tall = cols + 2 * GHOST
        dma = pltpu.SemaphoreType.DMA
        f32 = jnp.float32
        return pl.pallas_call(
            functools.partial(kernel, axes),
            out_shape=(jax.ShapeDtypeStruct(volt_now.shape, f32),) * 2,
            in_specs=[pl.BlockSpec(memory_space=pltpu.SMEM)] + [pl.BlockSpec(memory_space=pltpu.VMEM)] * 8,
            out_specs=(pl.BlockSpec(memory_space=pltpu.VMEM),) * 2,
            scratch_shapes=[
                pltpu.VMEM((5, axes[2], group, cols // 2, LANES), f32),
                pltpu.VMEM((5, layers, cols // 2, LANES), f32),
                pltpu.VMEM((8, layers, tall, LANES), f32),
                pltpu.VMEM((ITERS, layers, tall, LANES), f32),
                pltpu.VMEM((ITERS + 1, layers, tall, LANES), f32),
                pltpu.VMEM((5, 2, tall, LANES), f32),
                pltpu.VMEM((5, 2, tall, LANES), f32),
                pltpu.VMEM((cols, LANES), f32),
                pltpu.VMEM((2 * ITERS, TILE, LANES), f32),
                pltpu.VMEM((4, max(axes), 2 * ITERS, LANES), f32),
                pltpu.VMEM((2, axes[2], group, cols // 2, LANES), f32),
                pltpu.VMEM((2, axes[2], group, cols // 2, LANES), f32),
                dma((5,)), dma((5,)), dma((5,)),
                dma((5, 2)), dma((5, 2)), dma((5, 2)), dma((5, 2)),
                dma((3,)), dma((3,)), dma((2,)), dma((2,)), dma((2,)),
            ],
            compiler_params=pltpu.CompilerParams(
                collective_id=0, has_side_effects=True, vmem_limit_bytes=48 << 20
            ),
        )(current_table, volt_now, volt_prev, cap_term, edge_x, edge_y, via_below, cell_ids, placed)

    spec = P("al", "gx", "gy")
    return jax.shard_map(
        block,
        mesh=mesh,
        in_specs=(spec,) * 6 + (P("gx", "gy"), P("gx", "gy"), P()),
        out_specs=(spec, spec),
        check_vma=False,
    )
```

```python
import functools

import jax
import jax.numpy as jnp
from jax import lax
from jax.experimental import pallas as pl
from jax.experimental.pallas import tpu as pltpu
from jax.sharding import PartitionSpec as P

ITERS = 8
MESH = pl.DeviceIdType.MESH
EX, EY, VB, WI, UP, DN, EXL, EYL = range(8)
RHS = 4
GHOST = 8
TILE = 8
LANES = 128
AT_ONCE = 2
REFINE = 3


def rows_at(tile):
    return pl.ds(pl.multiple_of(tile * TILE, TILE), TILE)


def two_sum(a, b):
    s = a + b
    t = s - a
    return s, (a - (s - t)) + (b - t)


def pair_add(a, b):
    s, t = two_sum(a[0], b[0])
    t = t + (a[1] + b[1])
    high = s + t
    return high, t - (high - s)


def pair_less(a, b):
    return pair_add(a, (-b[0], -b[1]))


def scaled(power, a):
    return power * a[0], power * a[1]


def cut(a):
    t = 4097.0 * a
    high = t - (t - a)
    return high, a - high


def pair_times(a, b):
    p = a[0] * b[0]
    (ah, al), (bh, bl) = cut(a[0]), cut(b[0])
    t = ((ah * bh - p) + ah * bl + al * bh) + al * bl
    t = t + (a[0] * b[1] + a[1] * b[0])
    high = p + t
    return high, t - (high - p)


def kernel(
    axes, table, vn_h, vp_h, cap_h, ex_h, ey_h, vb_h, ids_h, placed_h, xo, ro,
    vn, vp, cap, ex, ey, vb, ids, placed, in_s, pack, recv, coef, s_buf, u_buf, ysend, yrecv, cur, part, gath, packo, recvo,
    t_ss, t_rs, l_s, x_ss, x_rs, y_ss, y_rs, r_ss, r_rs, o_ss, o_rs, lo_s,
):
    n_gx, n_gy, n_al = axes
    gx, gy, al = lax.axis_index("gx"), lax.axis_index("gy"), lax.axis_index("al")
    group, cols, rows = vn.shape
    layers = group * n_al
    width = rows // n_al
    half = cols // 2
    half_tiles = half // TILE
    own_tiles = cols // TILE
    tiles = own_tiles + 2
    odd = gy % 2
    strip = al * (1 - odd) + (n_al - 1 - al) * odd
    turn = 1 - 2 * odd

    def home(j):
        return j * (1 - odd) + (n_al - 1 - j) * odd

    at_hi = strip // (n_al - 1)
    at_lo = (n_al - 1 - strip) // (n_al - 1)
    right = {"gy": (gy + at_hi) % n_gy, "al": al + turn * (1 - at_hi)}
    left = {"gy": (gy + (n_gy - 1) * at_lo) % n_gy, "al": al - turn * (1 - at_lo)}
    fore = {"gx": (gx + 1) % n_gx}
    back = {"gx": (gx + n_gx - 1) % n_gx}
    al_peers = [{"al": (al + k) % n_al} for k in (4, 3, 5, 2, 6, 1, 7)]
    plane_peers = [
        {"gx": (gx + i) % n_gx, "gy": (gy + j) % n_gy}
        for i in (4, 5, 3, 2, 6, 7, 1, 0) for j in (2, 1, 3, 0) if i or j
    ]
    sum_groups = (plane_peers, al_peers)
    everyone = al_peers + plane_peers
    diagonal = [
        {"gx": (gx + i) % n_gx, "al": (al + j) % n_al} for i in (1, n_gx - 1) for j in (1, n_al - 1)
    ]

    barrier = pltpu.get_barrier_semaphore()
    for peer in everyone + diagonal:
        pl.semaphore_signal(barrier, inc=1, device_id=peer, device_id_type=MESH)
    reads = {
        name: pltpu.make_async_copy(src, dst, in_s.at[i])
        for i, (name, src, dst) in enumerate((
            (EX, ex_h, ex), (EY, ey_h, ey), (VB, vb_h, vb), (WI, cap_h, cap),
            ("vn", vn_h, vn), ("vp", vp_h, vp), ("ids", ids_h, ids), ("placed", placed_h, placed),
        ))
    }
    for copy in reads.values():
        copy.start()

    lane = lax.broadcasted_iota(jnp.int32, (TILE, LANES), 1)
    sub = lax.broadcasted_iota(jnp.int32, (TILE, LANES), 0)
    low = lane < width
    zero = jnp.zeros((TILE, LANES), jnp.float32)

    def value(which, layer, tile, q):
        at = (layer, rows_at(tile), pl.ds(q * LANES, LANES))
        if which == EX:
            last = (gx * cols + tile * TILE + sub) == n_gx * cols - 1
            return jnp.where(last, 0.0, ex[at])
        if which == EY:
            last = (gy * rows + q * LANES + lane) == n_gy * rows - 1
            return jnp.where(last, 0.0, ey[at])
        if which == VB:
            return jnp.where(al * group + layer == 0, 0.0, vb[at])
        if which == WI:
            return cap[at]
        return cap[at] * (4.0 * vn[at] - vp[at]) / 3.0

    def pack_array(which):
        for layer in range(group):
            def one(tile, c):
                for q in range(rows // LANES):
                    lo = value(which, layer, tile, q)
                    hi = value(which, layer, tile + half_tiles, q)
                    pack[which, 2 * q, layer, rows_at(tile)] = jnp.where(low, lo, pltpu.roll(hi, width, 1))
                    pack[which, 2 * q + 1, layer, rows_at(tile)] = jnp.where(low, pltpu.roll(lo, width, 1), hi)
                return c

            lax.fori_loop(0, half_tiles, one, 0)

    def own_copy(which):
        return pltpu.make_async_copy(
            pack.at[which, strip], recv.at[which, pl.ds(group * al, group)], l_s.at[which]
        )

    reads[EX].wait()
    pack_array(EX)
    pl.semaphore_wait(barrier, len(everyone + diagonal))
    for which in range(5):
        if which in (EY, VB, WI):
            reads[which].wait()
        if which == RHS:
            reads["vn"].wait()
            reads["vp"].wait()
        if which != EX:
            pack_array(which)
        for k in (4, 3, 5, 2, 6, 1, 7):
            to = (al + k) % n_al
            pltpu.make_async_remote_copy(
                src_ref=pack.at[which, home(to)],
                dst_ref=recv.at[which, pl.ds(group * al, group)],
                send_sem=t_ss.at[which],
                recv_sem=t_rs.at[which],
                device_id={"al": to},
                device_id_type=MESH,
            ).start()
        own_copy(which).start()

    def wait_array(which):
        many = recv.at[which, pl.ds(0, group * (n_al - 1))]
        pltpu.make_async_remote_copy(
            many, many, t_ss.at[which], t_rs.at[which], device_id={"al": al_peers[0]["al"]}, device_id_type=MESH
        ).wait_recv()
        own_copy(which).wait()

    mine = ids.at[:, pl.ds(pl.multiple_of((strip // 2) * LANES, LANES), LANES)]
    mine_placed = placed.at[:, pl.ds(pl.multiple_of((strip // 2) * LANES, LANES), LANES)]

    def stamp(tile, c):
        code = mine[rows_at(tile)]
        total = zero
        for kind in range(table.shape[0]):
            total = jnp.where(code == kind, table[kind], total)
        total = total * mine_placed[rows_at(tile)].astype(jnp.float32)
        total = jnp.where(strip % 2 == 0, total, pltpu.roll(total, width, 1))
        cur[rows_at(tile)] = jnp.where(low, total, 0.0)
        return c

    reads["ids"].wait()
    reads["placed"].wait()
    lax.fori_loop(0, own_tiles, stamp, 0)

    def unpack(which, dest):
        def one(tile, c):
            for layer in range(layers):
                v = recv[which, layer, rows_at(tile)]
                lo = jnp.where(low, v, 0.0)
                hi = jnp.where(low, pltpu.roll(v, width, 1), 0.0)
                if which == RHS and layer == 0:
                    lo = lo + cur[rows_at(tile)]
                    hi = hi + cur[rows_at(tile + half_tiles)]
                dest[layer, rows_at(tile + 1)] = lo
                dest[layer, rows_at(tile + 1 + half_tiles)] = hi
            return c

        lax.fori_loop(0, half_tiles, one, 0)

    def x_copies(which, dest):
        down = pltpu.make_async_remote_copy(
            dest.at[:, pl.ds(cols, GHOST)], dest.at[:, pl.ds(0, GHOST)],
            x_ss.at[which, 0], x_rs.at[which, 0], device_id=fore, device_id_type=MESH,
        )
        up = pltpu.make_async_remote_copy(
            dest.at[:, pl.ds(GHOST, GHOST)], dest.at[:, pl.ds(GHOST + cols, GHOST)],
            x_ss.at[which, 1], x_rs.at[which, 1], device_id=back, device_id_type=MESH,
        )
        return down, up

    def y_copies(which):
        out = []
        for way, peer in ((0, right), (1, left)):
            for part_of, across, src, dst in (
                (0, {}, pl.ds(GHOST, cols), pl.ds(GHOST, cols)),
                (1, fore, pl.ds(cols, GHOST), pl.ds(0, GHOST)),
                (2, back, pl.ds(GHOST, GHOST), pl.ds(GHOST + cols, GHOST)),
            ):
                out.append(
                    pltpu.make_async_remote_copy(
                        ysend.at[which, way, src], yrecv.at[which, way, dst],
                        y_ss.at[which, way, part_of], y_rs.at[which, way, part_of],
                        device_id={**peer, **across}, device_id_type=MESH,
                    )
                )
        return out

    def start_edges(which, dest):
        for copy in x_copies(which, dest):
            copy.start()

        def one(tile, c):
            to_right, to_left = zero, zero
            for layer in range(layers):
                here = lane // GHOST == layer
                v = dest[layer, rows_at(tile)]
                to_right = jnp.where(here, pltpu.roll(v, (GHOST * layer - (width - GHOST)) % LANES, 1), to_right)
                to_left = jnp.where(here, pltpu.roll(v, GHOST * layer, 1), to_left)
            ysend[which, 0, rows_at(tile)] = to_right
            ysend[which, 1, rows_at(tile)] = to_left
            return c

        lax.fori_loop(1, own_tiles + 1, one, 0)
        for copy in y_copies(which):
            copy.start()

    first = gy * n_al + strip == 0
    final = gy * n_al + strip == n_gy * n_al - 1

    def finish_edges(which, dest):
        for copy in x_copies(which, dest):
            copy.wait()
        for copy in y_copies(which):
            copy.wait()

        def one(tile, c):
            outside = jnp.logical_or(
                jnp.logical_and(gx == 0, tile == 0), jnp.logical_and(gx == n_gx - 1, tile == tiles - 1)
            )
            from_left = jnp.where(first, 0.0, yrecv[which, 0, rows_at(tile)])
            from_right = jnp.where(final, 0.0, yrecv[which, 1, rows_at(tile)])
            for layer in range(layers):
                v = dest[layer, rows_at(tile)]
                lft = pltpu.roll(from_left, (LANES - GHOST - GHOST * layer) % LANES, 1)
                rgt = pltpu.roll(from_right, (width - GHOST * layer) % LANES, 1)
                edge = jnp.where(lane < width + GHOST, rgt, jnp.where(lane >= LANES - GHOST, lft, 0.0))
                dest[layer, rows_at(tile)] = jnp.where(outside, 0.0, jnp.where(low, v, edge))
            return c

        lax.fori_loop(0, tiles, one, 0)

    def before(v, previous):
        return pltpu.roll(jnp.where(sub == TILE - 1, previous, v), 1, 0)

    def after(v, following):
        return pltpu.roll(jnp.where(sub == 0, following, v), TILE - 1, 0)

    u0 = u_buf.at[0]
    c_of = [coef.at[i] for i in range(8)]

    for which in (EX, EY, VB):
        wait_array(which)
        unpack(which, c_of[which])
        start_edges(which, c_of[which])
    finish_edges(EX, c_of[EX])
    finish_edges(EY, c_of[EY])

    def lefts(tile, c):
        above = jnp.maximum(tile - 1, 0)
        for layer in range(layers):
            coef[EXL, layer, rows_at(tile)] = before(coef[EX, layer, rows_at(tile)], coef[EX, layer, rows_at(above)])
            coef[EYL, layer, rows_at(tile)] = pltpu.roll(coef[EY, layer, rows_at(tile)], 1, 1)
        return c

    lax.fori_loop(0, tiles, lefts, 0)
    wait_array(WI)

    def pivots(tile, c):
        at = rows_at(tile + 1)
        upper = tile // half_tiles
        inverse = zero
        for layer in range(layers):
            held = recv[WI, layer, rows_at(tile % half_tiles)]
            held = jnp.where(upper == 0, held, pltpu.roll(held, width, 1))
            below = coef[VB, layer, at]
            diag = held + coef[EX, layer, at] + coef[EXL, layer, at] + coef[EY, layer, at] + coef[EYL, layer, at] + below
            if layer + 1 < layers:
                diag = diag + coef[VB, layer + 1, at]
            if layer:
                diag = diag - below * below * inverse
            inverse = jnp.where(low, 1.0 / diag, 0.0)
            coef[WI, layer, at] = inverse
        return c

    lax.fori_loop(0, own_tiles, pivots, 0)
    start_edges(WI, c_of[WI])
    finish_edges(VB, c_of[VB])
    wait_array(RHS)
    unpack(RHS, u0)
    start_edges(RHS, u0)
    finish_edges(WI, c_of[WI])

    def factors(tile, c):
        at = rows_at(tile)
        for layer in range(layers):
            inverse = coef[WI, layer, at]
            coef[UP, layer, at] = coef[VB, layer, at] * inverse
            if layer + 1 < layers:
                coef[DN, layer, at] = coef[VB, layer + 1, at] * inverse
        return c

    lax.fori_loop(0, tiles, factors, 0)
    finish_edges(RHS, u0)

    def solve(us, at):
        kept = []
        d = None
        for layer in range(layers):
            term = us[layer] * coef[WI, layer, at]
            d = term if layer == 0 else term + coef[UP, layer, at] * d
            kept.append(d)
        for layer in range(layers - 2, -1, -1):
            kept[layer] = kept[layer] + coef[DN, layer, at] * kept[layer + 1]
        return kept

    def is_own(tile):
        return jnp.logical_and(tile >= 1, tile <= own_tiles)

    def begin(turn_at, acc):
        for step in range(AT_ONCE):
            tile = turn_at * AT_ONCE + step
            at = rows_at(tile)
            us = [u_buf[0, layer, at] for layer in range(layers)]
            ss = solve(us, at)
            total = zero
            for layer in range(layers):
                s_buf[0, layer, at] = ss[layer]
                total = total + ss[layer] * us[layer]
            acc = acc + jnp.where(is_own(tile), total, 0.0)
        return acc

    part[0] = lax.fori_loop(0, tiles // AT_ONCE, begin, zero)

    def apply(k, onward):
        twice = jnp.where(k == 0, 1.0, 2.0)
        once = jnp.where(k == 0, 0.0, 1.0)
        older = jnp.maximum(k - 1, 0)

        def one(turn_at, accs):
            base = turn_at * AT_ONCE + (0 if onward else 1)
            ats = [rows_at(base + step) for step in range(AT_ONCE)]
            above = rows_at(jnp.maximum(base - 1, 0))
            under = rows_at(jnp.minimum(base + AT_ONCE, tiles - 1))
            cross = [zero] * AT_ONCE
            square = [zero] * AT_ONCE
            us = [[] for _ in ats]
            for layer in range(layers):
                vs = [s_buf[k, layer, at] for at in [above] + ats + [under]]
                for step, at in enumerate(ats):
                    v = vs[step + 1]
                    t = coef[EX, layer, at] * after(v, vs[step + 2]) + coef[EXL, layer, at] * before(v, vs[step])
                    t = t + (
                        coef[EY, layer, at] * pltpu.roll(v, LANES - 1, 1) + coef[EYL, layer, at] * pltpu.roll(v, 1, 1)
                    )
                    u = twice * t - once * u_buf[older, layer, at]
                    u_buf[k + 1, layer, at] = u
                    cross[step] = cross[step] + v * u
                    us[step].append(u)
            if onward:
                for step, at in enumerate(ats):
                    ss = solve(us[step], at)
                    for layer in range(layers):
                        s_buf[k + 1, layer, at] = ss[layer]
                        square[step] = square[step] + ss[layer] * us[step][layer]
            first_sum, second_sum = accs
            for step in range(AT_ONCE):
                own = is_own(base + step)
                first_sum = first_sum + jnp.where(own, cross[step], 0.0)
                second_sum = second_sum + jnp.where(own, square[step], 0.0)
            return first_sum, second_sum

        cross, square = lax.fori_loop(0, (tiles if onward else own_tiles) // AT_ONCE, one, (zero, zero))
        part[2 * k + 1] = cross
        if onward:
            part[2 * k + 2] = square

    def steps(k, c):
        apply(k, True)
        return c

    lax.fori_loop(0, ITERS - 1, steps, 0)
    apply(ITERS - 1, False)

    n_sums = 2 * ITERS
    rowed = lax.broadcasted_iota(jnp.int32, (n_sums, LANES), 0)
    laned = lax.broadcasted_iota(jnp.int32, (n_sums, LANES), 1)

    def halved(high, low_part, axis):
        while high.shape[axis] > 1:
            n = high.shape[axis] // 2
            a = lax.slice_in_dim(high, 0, n, axis=axis), lax.slice_in_dim(low_part, 0, n, axis=axis)
            b = lax.slice_in_dim(high, n, 2 * n, axis=axis), lax.slice_in_dim(low_part, n, 2 * n, axis=axis)
            high, low_part = pair_add(a, b)
        return high, low_part

    def turned(high, low_part, length, axis):
        shift = length // 2
        while shift:
            high, low_part = pair_add(
                (high, low_part), (pltpu.roll(high, shift, axis), pltpu.roll(low_part, shift, axis))
            )
            shift //= 2
        return high, low_part

    total = halved(*[jnp.where(low[None], part[...], 0.0), jnp.zeros_like(part)], 1)
    total = turned(total[0][:, 0], total[1][:, 0], LANES, 1)
    here = laned == rowed
    line = jnp.sum(jnp.where(here, total[0], 0.0), axis=0, keepdims=True) + jnp.sum(
        jnp.where(laned == rowed + LANES // 2, total[1], 0.0), axis=0, keepdims=True
    )
    for stage, peers in enumerate(sum_groups):
        count = len(peers) + 1
        gath[stage, pl.ds(count - 1, 1)] = line
        for slot, peer in enumerate(peers):
            pltpu.make_async_remote_copy(
                gath.at[stage, pl.ds(count - 1, 1)], gath.at[stage, pl.ds(slot, 1)], r_ss.at[stage], r_rs.at[stage],
                device_id=peer, device_id_type=MESH,
            ).start()
        many = gath.at[stage, pl.ds(0, count - 1)]
        pltpu.make_async_remote_copy(
            many, many, r_ss.at[stage], r_rs.at[stage], device_id=peers[0], device_id_type=MESH
        ).wait()
        got = gath[stage, 0:count]
        got_low = pltpu.roll(got, LANES // 2, 1)
        high, low_part = got[0:TILE], got_low[0:TILE]
        for i in range(1, count // TILE):
            high, low_part = pair_add(
                (high, low_part), (got[i * TILE : (i + 1) * TILE], got_low[i * TILE : (i + 1) * TILE])
            )
        high, low_part = turned(high, low_part, TILE, 0)
        line = jnp.where(low, high, pltpu.roll(low_part, LANES // 2, 1))[0:1]
    spread = jnp.broadcast_to(line, (n_sums, LANES))
    highs = jnp.broadcast_to(jnp.sum(jnp.where(here, spread, 0.0), axis=1, keepdims=True), (n_sums, LANES))
    lows = jnp.broadcast_to(
        jnp.sum(jnp.where(laned == rowed + LANES // 2, spread, 0.0), axis=1, keepdims=True), (n_sums, LANES)
    )

    def splat(array, i):
        return jnp.broadcast_to(array[i : i + 1], (TILE, LANES))

    pair = [(splat(highs, i), splat(lows, i)) for i in range(n_sums)]
    moment = [pair[0], pair[1]]
    for i in range(2, n_sums):
        moment.append(pair_less(scaled(2.0, pair[i]), pair[i % 2]))
    q = [pair_less(moment[0], moment[1])]
    for i in range(1, n_sums - 1):
        q.append(pair_less(moment[i], scaled(0.5, pair_add(moment[i + 1], moment[i - 1]))))

    def stacked(parts):
        out = parts[0]
        for i in range(1, ITERS):
            out = jnp.where(sub == i, parts[i], out)
        return out

    def column(j, which):
        return stacked([q[i + j][which] for i in range(ITERS)]), stacked([q[abs(i - j)][which] for i in range(ITERS)])

    mat = []
    for j in range(ITERS):
        (high_a, high_b), (low_a, low_b) = column(j, 0), column(j, 1)
        mat.append(scaled(0.5, pair_add((high_a, low_a), (high_b, low_b))))
    vec = (stacked([moment[i][0] for i in range(ITERS)]), stacked([moment[i][1] for i in range(ITERS)]))

    left_over = [m[0] for m in mat]
    lower, inv = [], []
    for k in range(ITERS):
        inv.append(1.0 / splat(left_over[k], k))
        lower.append(jnp.where(sub > k, left_over[k] * inv[k], 0.0))
        for j in range(k + 1, ITERS):
            left_over[j] = left_over[j] - lower[k] * splat(left_over[j], k)

    def solved(right_side):
        for k in range(ITERS - 1):
            right_side = right_side - lower[k] * splat(right_side, k)
        out = [None] * ITERS
        for k in range(ITERS - 1, -1, -1):
            out[k] = splat(right_side, k) * inv[k]
            right_side = right_side - jnp.where(sub < k, left_over[k], 0.0) * out[k]
        return out

    c = [(a, zero) for a in solved(vec[0])]
    for _ in range(REFINE):
        rest = vec
        for j in range(ITERS):
            rest = pair_less(rest, pair_times(mat[j], c[j]))
        c = [pair_add(a, (b, zero)) for a, b in zip(c, solved(rest[0]))]
    e = []
    for n in range(ITERS + 1):
        total = (jnp.ones_like(zero), zero) if n == 0 else (zero, zero)
        if n < ITERS:
            total = pair_less(total, c[n])
        if n >= 1:
            total = pair_add(total, c[0] if n == 1 else scaled(0.5, c[n - 1]))
        if n + 1 < ITERS:
            total = pair_add(total, scaled(0.5, c[n + 1]))
        e.append(total[0])
    cs = [a[0] for a in c]
    es = e

    def out_copy(which, to):
        return pltpu.make_async_remote_copy(
            packo.at[which, to], recvo.at[which, strip], o_ss.at[which], o_rs.at[which],
            device_id={"al": to}, device_id_type=MESH,
        )

    def combine(buf, weights, layer, tile):
        at = rows_at(tile)
        total = weights[0] * buf[0, layer, at]
        for j in range(1, len(weights)):
            total = total + weights[j] * buf[j, layer, at]
        return total

    for k in (4, 3, 5, 2, 6, 1, 7, 0):
        to = (al + k) % n_al
        for which, buf, weights in ((0, s_buf, cs), (1, u_buf, es)):
            for member in range(group):
                layer = to * group + member

                def one(tile, carry):
                    lo = combine(buf, weights, layer, tile + 1)
                    hi = combine(buf, weights, layer, tile + 1 + half_tiles)
                    packo[which, to, member, rows_at(tile)] = jnp.where(low, lo, pltpu.roll(hi, width, 1))
                    return carry

                lax.fori_loop(0, half_tiles, one, 0)
            if k:
                out_copy(which, to).start()
            else:
                pltpu.make_async_copy(packo.at[which, al], recvo.at[which, strip], lo_s.at[which]).start()

    for which, dest in ((0, xo), (1, ro)):
        many = recvo.at[which, pl.ds(0, n_al - 1)]
        pltpu.make_async_remote_copy(
            many, many, o_ss.at[which], o_rs.at[which], device_id=al_peers[0], device_id_type=MESH
        ).wait()
        pltpu.make_async_copy(packo.at[which, al], recvo.at[which, strip], lo_s.at[which]).wait()

        def one(tile, carry):
            for member in range(group):
                for tq in range(rows // LANES):
                    p = recvo[which, 2 * tq, member, rows_at(tile)]
                    r = recvo[which, 2 * tq + 1, member, rows_at(tile)]
                    dest[member, rows_at(tile), pl.ds(tq * LANES, LANES)] = jnp.where(low, p, pltpu.roll(r, width, 1))
                    dest[member, rows_at(tile + half_tiles), pl.ds(tq * LANES, LANES)] = jnp.where(
                        low, pltpu.roll(p, width, 1), r
                    )
            return carry

        lax.fori_loop(0, half_tiles, one, 0)

    for which in range(5):
        many = recv.at[which, pl.ds(0, group * (n_al - 1))]
        pltpu.make_async_remote_copy(
            many, many, t_ss.at[which], t_rs.at[which], device_id=al_peers[0], device_id_type=MESH
        ).wait_send()


def solution(mesh):
    axes = (mesh.shape["gx"], mesh.shape["gy"], mesh.shape["al"])

    def block(volt_now, volt_prev, cap_term, edge_x, edge_y, via_below, cell_ids, placed, current_table):
        group, cols, rows = volt_now.shape
        layers = group * axes[2]
        tall = cols + 2 * GHOST
        dma = pltpu.SemaphoreType.DMA
        f32 = jnp.float32
        return pl.pallas_call(
            functools.partial(kernel, axes),
            out_shape=(jax.ShapeDtypeStruct(volt_now.shape, f32),) * 2,
            in_specs=[pl.BlockSpec(memory_space=pltpu.SMEM)] + [pl.BlockSpec(memory_space=pl.ANY)] * 8,
            out_specs=(pl.BlockSpec(memory_space=pltpu.VMEM),) * 2,
            scratch_shapes=[pltpu.VMEM(volt_now.shape, f32)] * 6 + [pltpu.VMEM(cell_ids.shape, jnp.int32)] * 2 + [
                dma((8,)),
                pltpu.VMEM((5, axes[2], group, cols // 2, LANES), f32),
                pltpu.VMEM((5, layers, cols // 2, LANES), f32),
                pltpu.VMEM((8, layers, tall, LANES), f32),
                pltpu.VMEM((ITERS, layers, tall, LANES), f32),
                pltpu.VMEM((ITERS + 1, layers, tall, LANES), f32),
                pltpu.VMEM((5, 2, tall, LANES), f32),
                pltpu.VMEM((5, 2, tall, LANES), f32),
                pltpu.VMEM((cols, LANES), f32),
                pltpu.VMEM((2 * ITERS, TILE, LANES), f32),
                pltpu.VMEM((2, axes[0] * axes[1], LANES), f32),
                pltpu.VMEM((2, axes[2], group, cols // 2, LANES), f32),
                pltpu.VMEM((2, axes[2], group, cols // 2, LANES), f32),
                dma((5,)), dma((5,)), dma((5,)),
                dma((5, 2)), dma((5, 2)), dma((5, 2, 3)), dma((5, 2, 3)),
                dma((3,)), dma((3,)), dma((2,)), dma((2,)), dma((2,)),
            ],
            compiler_params=pltpu.CompilerParams(
                collective_id=0, has_side_effects=True, vmem_limit_bytes=60 << 20
            ),
        )(current_table, volt_now, volt_prev, cap_term, edge_x, edge_y, via_below, cell_ids, placed)

    spec = P("al", "gx", "gy")
    return jax.shard_map(
        block,
        mesh=mesh,
        in_specs=(spec,) * 6 + (P("gx", "gy"), P("gx", "gy"), P()),
        out_specs=(spec, spec),
        check_vma=False,
    )
```

```python
import functools

import jax
import jax.numpy as jnp
from jax import lax
from jax.experimental import pallas as pl
from jax.experimental.pallas import tpu as pltpu
from jax.sharding import PartitionSpec as P

ITERS = 8
MESH = pl.DeviceIdType.MESH
EX, EY, VB, WI, UP, DN, EXL, EYL = range(8)
RHS = 4
GHOST = 8
TILE = 8
LANES = 128
AT_ONCE = 5
REFINE = 3


def rows_at(tile):
    return pl.ds(pl.multiple_of(tile * TILE, TILE), TILE)


def two_sum(a, b):
    s = a + b
    t = s - a
    return s, (a - (s - t)) + (b - t)


def pair_add(a, b):
    s, t = two_sum(a[0], b[0])
    t = t + (a[1] + b[1])
    high = s + t
    return high, t - (high - s)


def pair_less(a, b):
    return pair_add(a, (-b[0], -b[1]))


def scaled(power, a):
    return power * a[0], power * a[1]


def cut(a):
    t = 4097.0 * a
    high = t - (t - a)
    return high, a - high


def pair_times(a, b):
    p = a[0] * b[0]
    (ah, al), (bh, bl) = cut(a[0]), cut(b[0])
    t = ((ah * bh - p) + ah * bl + al * bh) + al * bl
    t = t + (a[0] * b[1] + a[1] * b[0])
    high = p + t
    return high, t - (high - p)


def kernel(
    axes, table, vn_h, vp_h, cap_h, ex_h, ey_h, vb_h, ids_h, placed_h, xo, ro,
    vn, vp, cap, ex, ey, vb, ids, placed, in_s, pack, recv, coef, s_buf, u_buf, ysend, yrecv, cur, middle, part, gath, packo, recvo,
    t_ss, t_rs, l_s, x_ss, x_rs, y_ss, y_rs, r_ss, r_rs, o_ss, o_rs, lo_s,
):
    n_gx, n_gy, n_al = axes
    gx, gy, al = lax.axis_index("gx"), lax.axis_index("gy"), lax.axis_index("al")
    group, cols, rows = vn.shape
    layers = group * n_al
    width = rows // n_al
    half = cols // 2
    half_tiles = half // TILE
    own_tiles = cols // TILE
    tiles = own_tiles + 2
    odd = gy % 2
    strip = al * (1 - odd) + (n_al - 1 - al) * odd
    turn = 1 - 2 * odd

    def home(j):
        return j * (1 - odd) + (n_al - 1 - j) * odd

    at_hi = strip // (n_al - 1)
    at_lo = (n_al - 1 - strip) // (n_al - 1)
    right = {"gy": (gy + at_hi) % n_gy, "al": al + turn * (1 - at_hi)}
    left = {"gy": (gy + (n_gy - 1) * at_lo) % n_gy, "al": al - turn * (1 - at_lo)}
    fore = {"gx": (gx + 1) % n_gx}
    back = {"gx": (gx + n_gx - 1) % n_gx}
    al_peers = [{"al": (al + k) % n_al} for k in (4, 3, 5, 2, 6, 1, 7)]
    plane_peers = [
        {"gx": (gx + i) % n_gx, "gy": (gy + j) % n_gy}
        for i in (4, 5, 3, 2, 6, 7, 1, 0) for j in (2, 1, 3, 0) if i or j
    ]
    sum_groups = (plane_peers, al_peers)
    everyone = al_peers + plane_peers
    diagonal = [
        {"gx": (gx + i) % n_gx, "al": (al + j) % n_al} for i in (1, n_gx - 1) for j in (1, n_al - 1)
    ]

    barrier = pltpu.get_barrier_semaphore()
    for peer in everyone + diagonal:
        pl.semaphore_signal(barrier, inc=1, device_id=peer, device_id_type=MESH)
    reads = {
        name: pltpu.make_async_copy(src, dst, in_s.at[i])
        for i, (name, src, dst) in enumerate((
            (EX, ex_h, ex), (EY, ey_h, ey), (VB, vb_h, vb), (WI, cap_h, cap),
            ("vn", vn_h, vn), ("vp", vp_h, vp), ("ids", ids_h, ids), ("placed", placed_h, placed),
        ))
    }
    for copy in reads.values():
        copy.start()

    lane = lax.broadcasted_iota(jnp.int32, (TILE, LANES), 1)
    sub = lax.broadcasted_iota(jnp.int32, (TILE, LANES), 0)
    low = lane < width
    zero = jnp.zeros((TILE, LANES), jnp.float32)

    def value(which, layer, tile, q):
        at = (layer, rows_at(tile), pl.ds(q * LANES, LANES))
        if which == EX:
            last = (gx * cols + tile * TILE + sub) == n_gx * cols - 1
            return jnp.where(last, 0.0, ex[at])
        if which == EY:
            last = (gy * rows + q * LANES + lane) == n_gy * rows - 1
            return jnp.where(last, 0.0, ey[at])
        if which == VB:
            return jnp.where(al * group + layer == 0, 0.0, vb[at])
        if which == WI:
            return cap[at]
        return cap[at] * (4.0 * vn[at] - vp[at]) / 3.0

    def pack_array(which):
        for layer in range(group):
            def one(tile, c):
                for q in range(rows // LANES):
                    lo = value(which, layer, tile, q)
                    hi = value(which, layer, tile + half_tiles, q)
                    pack[which, 2 * q, layer, rows_at(tile)] = jnp.where(low, lo, pltpu.roll(hi, width, 1))
                    pack[which, 2 * q + 1, layer, rows_at(tile)] = jnp.where(low, pltpu.roll(lo, width, 1), hi)
                return c

            lax.fori_loop(0, half_tiles, one, 0)

    def own_copy(which):
        return pltpu.make_async_copy(
            pack.at[which, strip], recv.at[which, pl.ds(group * al, group)], l_s.at[which]
        )

    reads[EX].wait()
    pack_array(EX)
    pl.semaphore_wait(barrier, len(everyone + diagonal))
    for which in range(5):
        if which in (EY, VB, WI):
            reads[which].wait()
        if which == RHS:
            reads["vn"].wait()
            reads["vp"].wait()
        if which != EX:
            pack_array(which)
        for k in (4, 3, 5, 2, 6, 1, 7):
            to = (al + k) % n_al
            pltpu.make_async_remote_copy(
                src_ref=pack.at[which, home(to)],
                dst_ref=recv.at[which, pl.ds(group * al, group)],
                send_sem=t_ss.at[which],
                recv_sem=t_rs.at[which],
                device_id={"al": to},
                device_id_type=MESH,
            ).start()
        own_copy(which).start()

    def wait_array(which):
        many = recv.at[which, pl.ds(0, group * (n_al - 1))]
        pltpu.make_async_remote_copy(
            many, many, t_ss.at[which], t_rs.at[which], device_id={"al": al_peers[0]["al"]}, device_id_type=MESH
        ).wait_recv()
        own_copy(which).wait()

    mine = ids.at[:, pl.ds(pl.multiple_of((strip // 2) * LANES, LANES), LANES)]
    mine_placed = placed.at[:, pl.ds(pl.multiple_of((strip // 2) * LANES, LANES), LANES)]

    def stamp(tile, c):
        code = mine[rows_at(tile)]
        total = zero
        for kind in range(table.shape[0]):
            total = jnp.where(code == kind, table[kind], total)
        total = total * mine_placed[rows_at(tile)].astype(jnp.float32)
        total = jnp.where(strip % 2 == 0, total, pltpu.roll(total, width, 1))
        cur[rows_at(tile)] = jnp.where(low, total, 0.0)
        return c

    reads["ids"].wait()
    reads["placed"].wait()
    lax.fori_loop(0, own_tiles, stamp, 0)

    def unpack(which, dest):
        def one(tile, c):
            for layer in range(layers):
                v = recv[which, layer, rows_at(tile)]
                lo = jnp.where(low, v, 0.0)
                hi = jnp.where(low, pltpu.roll(v, width, 1), 0.0)
                if which == RHS and layer == 0:
                    lo = lo + cur[rows_at(tile)]
                    hi = hi + cur[rows_at(tile + half_tiles)]
                dest[layer, rows_at(tile + 1)] = lo
                dest[layer, rows_at(tile + 1 + half_tiles)] = hi
            return c

        lax.fori_loop(0, half_tiles, one, 0)

    def x_copies(which, dest):
        down = pltpu.make_async_remote_copy(
            dest.at[:, pl.ds(cols, GHOST)], dest.at[:, pl.ds(0, GHOST)],
            x_ss.at[which, 0], x_rs.at[which, 0], device_id=fore, device_id_type=MESH,
        )
        up = pltpu.make_async_remote_copy(
            dest.at[:, pl.ds(GHOST, GHOST)], dest.at[:, pl.ds(GHOST + cols, GHOST)],
            x_ss.at[which, 1], x_rs.at[which, 1], device_id=back, device_id_type=MESH,
        )
        return down, up

    def y_copies(which):
        out = []
        for way, peer in ((0, right), (1, left)):
            for part_of, across, src, dst in (
                (0, {}, pl.ds(GHOST, cols), pl.ds(GHOST, cols)),
                (1, fore, pl.ds(cols, GHOST), pl.ds(0, GHOST)),
                (2, back, pl.ds(GHOST, GHOST), pl.ds(GHOST + cols, GHOST)),
            ):
                out.append(
                    pltpu.make_async_remote_copy(
                        ysend.at[which, way, src], yrecv.at[which, way, dst],
                        y_ss.at[which, way, part_of], y_rs.at[which, way, part_of],
                        device_id={**peer, **across}, device_id_type=MESH,
                    )
                )
        return out

    def start_edges(which, dest):
        for copy in x_copies(which, dest):
            copy.start()

        def one(tile, c):
            to_right, to_left = zero, zero
            for layer in range(layers):
                here = lane // GHOST == layer
                v = dest[layer, rows_at(tile)]
                to_right = jnp.where(here, pltpu.roll(v, (GHOST * layer - (width - GHOST)) % LANES, 1), to_right)
                to_left = jnp.where(here, pltpu.roll(v, GHOST * layer, 1), to_left)
            ysend[which, 0, rows_at(tile)] = to_right
            ysend[which, 1, rows_at(tile)] = to_left
            return c

        lax.fori_loop(1, own_tiles + 1, one, 0)
        for copy in y_copies(which):
            copy.start()

    first = gy * n_al + strip == 0
    final = gy * n_al + strip == n_gy * n_al - 1

    def finish_edges(which, dest):
        for copy in x_copies(which, dest):
            copy.wait()
        for copy in y_copies(which):
            copy.wait()

        def one(tile, c):
            outside = jnp.logical_or(
                jnp.logical_and(gx == 0, tile == 0), jnp.logical_and(gx == n_gx - 1, tile == tiles - 1)
            )
            from_left = jnp.where(first, 0.0, yrecv[which, 0, rows_at(tile)])
            from_right = jnp.where(final, 0.0, yrecv[which, 1, rows_at(tile)])
            for layer in range(layers):
                v = dest[layer, rows_at(tile)]
                lft = pltpu.roll(from_left, (LANES - GHOST - GHOST * layer) % LANES, 1)
                rgt = pltpu.roll(from_right, (width - GHOST * layer) % LANES, 1)
                edge = jnp.where(lane < width + GHOST, rgt, jnp.where(lane >= LANES - GHOST, lft, 0.0))
                dest[layer, rows_at(tile)] = jnp.where(outside, 0.0, jnp.where(low, v, edge))
            return c

        lax.fori_loop(0, tiles, one, 0)

    def before(v, previous):
        return pltpu.roll(jnp.where(sub == TILE - 1, previous, v), 1, 0)

    def after(v, following):
        return pltpu.roll(jnp.where(sub == 0, following, v), TILE - 1, 0)

    u0 = u_buf.at[0]
    c_of = [coef.at[i] for i in range(8)]

    for which in (EX, EY, VB):
        wait_array(which)
        unpack(which, c_of[which])
        start_edges(which, c_of[which])
    wait_array(WI)

    def sums_at_home(tile, c):
        at = rows_at(tile + 1)
        above = rows_at(jnp.maximum(tile, 1))
        upper = tile // half_tiles
        inner = jnp.logical_or(tile > 0, sub > 0)
        for layer in range(layers):
            held = recv[WI, layer, rows_at(tile % half_tiles)]
            held = jnp.where(upper == 0, held, pltpu.roll(held, width, 1))
            x, y = coef[EX, layer, at], coef[EY, layer, at]
            held = held + (x + jnp.where(inner, before(x, coef[EX, layer, above]), 0.0)) + (y + pltpu.roll(y, 1, 1))
            coef[WI, layer, at] = jnp.where(low, held, 0.0)
        return c

    lax.fori_loop(0, own_tiles, sums_at_home, 0)
    start_edges(WI, c_of[WI])
    wait_array(RHS)
    unpack(RHS, u0)
    start_edges(RHS, u0)
    finish_edges(EX, c_of[EX])
    finish_edges(EY, c_of[EY])

    def lefts(tile, c):
        above = jnp.maximum(tile - 1, 0)
        for layer in range(layers):
            coef[EXL, layer, rows_at(tile)] = before(coef[EX, layer, rows_at(tile)], coef[EX, layer, rows_at(above)])
            coef[EYL, layer, rows_at(tile)] = pltpu.roll(coef[EY, layer, rows_at(tile)], 1, 1)
        return c

    lax.fori_loop(0, tiles, lefts, 0)
    finish_edges(VB, c_of[VB])
    finish_edges(WI, c_of[WI])

    def pivots(turn_at, c):
        each = [turn_at * AT_ONCE + step for step in range(AT_ONCE)]
        mid = layers // 2
        met = {}
        for step, tile in enumerate(each):
            at = rows_at(tile)
            seam = jnp.logical_and(sub == 0, jnp.logical_or(tile == 1, tile == tiles - 1))
            edge = jnp.logical_or(lane == 0, lane == width)
            for rank in range(mid):
                for layer, previous in ((rank, rank - 1), (layers - 1 - rank, layers - rank)):
                    held = coef[WI, layer, at]
                    below = coef[VB, layer, at]
                    over = coef[VB, layer + 1, at] if layer + 1 < layers else zero
                    diag = held + jnp.where(seam, coef[EXL, layer, at], 0.0)
                    diag = diag + jnp.where(edge, coef[EYL, layer, at], 0.0)
                    diag = diag + (below + over)
                    if rank:
                        link = below if previous < layer else over
                        diag = diag - link * (link * met[step, previous])
                    inverse = jnp.where(held > 0.0, 1.0 / diag, 0.0)
                    met[step, layer] = inverse
                    coef[WI, layer, at] = inverse
                    coef[UP, layer, at] = below * inverse
                    coef[DN, layer, at] = over * inverse
            link = coef[VB, mid, at]
            middle[at] = 1.0 / (1.0 - (link * met[step, mid - 1]) * (link * met[step, mid]))
        return c

    lax.fori_loop(0, tiles // AT_ONCE, pivots, 0)
    finish_edges(RHS, u0)

    def solve(us, at):
        mid = layers // 2
        kept = [us[layer] * coef[WI, layer, at] for layer in range(layers)]
        for rank in range(1, mid):
            lo, hi = rank, layers - 1 - rank
            kept[lo] = kept[lo] + coef[UP, lo, at] * kept[lo - 1]
            kept[hi] = kept[hi] + coef[DN, hi, at] * kept[hi + 1]
        kept[mid - 1] = middle[at] * (kept[mid - 1] + coef[DN, mid - 1, at] * kept[mid])
        kept[mid] = kept[mid] + coef[UP, mid, at] * kept[mid - 1]
        for rank in range(mid - 2, -1, -1):
            lo, hi = rank, layers - 1 - rank
            kept[lo] = kept[lo] + coef[DN, lo, at] * kept[lo + 1]
            kept[hi] = kept[hi] + coef[UP, hi, at] * kept[hi - 1]
        return kept

    def is_own(tile):
        return jnp.logical_and(tile >= 1, tile <= own_tiles)

    def begin(turn_at, acc):
        for step in range(AT_ONCE):
            tile = turn_at * AT_ONCE + step
            at = rows_at(tile)
            us = [u_buf[0, layer, at] for layer in range(layers)]
            ss = solve(us, at)
            total = zero
            for layer in range(layers):
                s_buf[0, layer, at] = ss[layer]
                total = total + ss[layer] * us[layer]
            acc = acc + jnp.where(is_own(tile), total, 0.0)
        return acc

    part[0] = lax.fori_loop(0, tiles // AT_ONCE, begin, zero)

    def apply(k, onward):
        at_once = 5 if onward else 4
        twice = jnp.where(k == 0, 1.0, 2.0)
        once = jnp.where(k == 0, 0.0, 1.0)
        older = jnp.maximum(k - 1, 0)

        def one(turn_at, accs):
            base = turn_at * at_once + (0 if onward else 1)
            ats = [rows_at(base + step) for step in range(at_once)]
            above = rows_at(jnp.maximum(base - 1, 0))
            under = rows_at(jnp.minimum(base + at_once, tiles - 1))
            cross = [zero] * at_once
            square = [zero] * at_once
            us = [[] for _ in ats]
            for layer in range(layers):
                vs = [s_buf[k, layer, at] for at in [above] + ats + [under]]
                for step, at in enumerate(ats):
                    v = vs[step + 1]
                    t = coef[EX, layer, at] * after(v, vs[step + 2]) + coef[EXL, layer, at] * before(v, vs[step])
                    t = t + (
                        coef[EY, layer, at] * pltpu.roll(v, LANES - 1, 1) + coef[EYL, layer, at] * pltpu.roll(v, 1, 1)
                    )
                    u = twice * t - once * u_buf[older, layer, at]
                    u_buf[k + 1, layer, at] = u
                    cross[step] = cross[step] + v * u
                    us[step].append(u)
            if onward:
                for step, at in enumerate(ats):
                    ss = solve(us[step], at)
                    for layer in range(layers):
                        s_buf[k + 1, layer, at] = ss[layer]
                        square[step] = square[step] + ss[layer] * us[step][layer]
            first_sum, second_sum = accs
            for step in range(at_once):
                own = is_own(base + step)
                first_sum = first_sum + jnp.where(own, cross[step], 0.0)
                second_sum = second_sum + jnp.where(own, square[step], 0.0)
            return first_sum, second_sum

        cross, square = lax.fori_loop(0, (tiles if onward else own_tiles) // at_once, one, (zero, zero))
        part[2 * k + 1] = cross
        if onward:
            part[2 * k + 2] = square

    def steps(k, c):
        apply(k, True)
        return c

    lax.fori_loop(0, ITERS - 1, steps, 0)
    apply(ITERS - 1, False)

    n_sums = 2 * ITERS
    rowed = lax.broadcasted_iota(jnp.int32, (n_sums, LANES), 0)
    laned = lax.broadcasted_iota(jnp.int32, (n_sums, LANES), 1)

    def halved(high, low_part, axis):
        while high.shape[axis] > 1:
            n = high.shape[axis] // 2
            a = lax.slice_in_dim(high, 0, n, axis=axis), lax.slice_in_dim(low_part, 0, n, axis=axis)
            b = lax.slice_in_dim(high, n, 2 * n, axis=axis), lax.slice_in_dim(low_part, n, 2 * n, axis=axis)
            high, low_part = pair_add(a, b)
        return high, low_part

    def turned(high, low_part, length, axis):
        shift = length // 2
        while shift:
            high, low_part = pair_add(
                (high, low_part), (pltpu.roll(high, shift, axis), pltpu.roll(low_part, shift, axis))
            )
            shift //= 2
        return high, low_part

    total = halved(*[jnp.where(low[None], part[...], 0.0), jnp.zeros_like(part)], 1)
    total = turned(total[0][:, 0], total[1][:, 0], LANES, 1)
    here = laned == rowed
    line = jnp.sum(jnp.where(here, total[0], 0.0), axis=0, keepdims=True) + jnp.sum(
        jnp.where(laned == rowed + LANES // 2, total[1], 0.0), axis=0, keepdims=True
    )
    for stage, peers in enumerate(sum_groups):
        count = len(peers) + 1
        gath[stage, pl.ds(count - 1, 1)] = line
        for slot, peer in enumerate(peers):
            pltpu.make_async_remote_copy(
                gath.at[stage, pl.ds(count - 1, 1)], gath.at[stage, pl.ds(slot, 1)], r_ss.at[stage], r_rs.at[stage],
                device_id=peer, device_id_type=MESH,
            ).start()
        many = gath.at[stage, pl.ds(0, count - 1)]
        pltpu.make_async_remote_copy(
            many, many, r_ss.at[stage], r_rs.at[stage], device_id=peers[0], device_id_type=MESH
        ).wait()
        got = gath[stage, 0:count]
        got_low = pltpu.roll(got, LANES // 2, 1)
        high, low_part = got[0:TILE], got_low[0:TILE]
        for i in range(1, count // TILE):
            high, low_part = pair_add(
                (high, low_part), (got[i * TILE : (i + 1) * TILE], got_low[i * TILE : (i + 1) * TILE])
            )
        high, low_part = turned(high, low_part, TILE, 0)
        line = jnp.where(low, high, pltpu.roll(low_part, LANES // 2, 1))[0:1]
    spread = jnp.broadcast_to(line, (n_sums, LANES))
    highs = jnp.broadcast_to(jnp.sum(jnp.where(here, spread, 0.0), axis=1, keepdims=True), (n_sums, LANES))
    lows = jnp.broadcast_to(
        jnp.sum(jnp.where(laned == rowed + LANES // 2, spread, 0.0), axis=1, keepdims=True), (n_sums, LANES)
    )

    def splat(array, i):
        return jnp.broadcast_to(array[i : i + 1], (TILE, LANES))

    pair = [(splat(highs, i), splat(lows, i)) for i in range(n_sums)]
    moment = [pair[0], pair[1]]
    for i in range(2, n_sums):
        moment.append(pair_less(scaled(2.0, pair[i]), pair[i % 2]))
    q = [pair_less(moment[0], moment[1])]
    for i in range(1, n_sums - 1):
        q.append(pair_less(moment[i], scaled(0.5, pair_add(moment[i + 1], moment[i - 1]))))

    def stacked(parts):
        out = parts[0]
        for i in range(1, ITERS):
            out = jnp.where(sub == i, parts[i], out)
        return out

    def column(j, which):
        return stacked([q[i + j][which] for i in range(ITERS)]), stacked([q[abs(i - j)][which] for i in range(ITERS)])

    mat = []
    for j in range(ITERS):
        (high_a, high_b), (low_a, low_b) = column(j, 0), column(j, 1)
        mat.append(scaled(0.5, pair_add((high_a, low_a), (high_b, low_b))))
    vec = (stacked([moment[i][0] for i in range(ITERS)]), stacked([moment[i][1] for i in range(ITERS)]))

    left_over = [m[0] for m in mat]
    lower, inv = [], []
    for k in range(ITERS):
        inv.append(1.0 / splat(left_over[k], k))
        lower.append(jnp.where(sub > k, left_over[k] * inv[k], 0.0))
        for j in range(k + 1, ITERS):
            left_over[j] = left_over[j] - lower[k] * splat(left_over[j], k)

    def solved(right_side):
        for k in range(ITERS - 1):
            right_side = right_side - lower[k] * splat(right_side, k)
        out = [None] * ITERS
        for k in range(ITERS - 1, -1, -1):
            out[k] = splat(right_side, k) * inv[k]
            right_side = right_side - jnp.where(sub < k, left_over[k], 0.0) * out[k]
        return out

    c = [(a, zero) for a in solved(vec[0])]
    for _ in range(REFINE):
        rest = vec
        for j in range(ITERS):
            rest = pair_less(rest, pair_times(mat[j], c[j]))
        c = [pair_add(a, (b, zero)) for a, b in zip(c, solved(rest[0]))]
    e = []
    for n in range(ITERS + 1):
        total = (jnp.ones_like(zero), zero) if n == 0 else (zero, zero)
        if n < ITERS:
            total = pair_less(total, c[n])
        if n >= 1:
            total = pair_add(total, c[0] if n == 1 else scaled(0.5, c[n - 1]))
        if n + 1 < ITERS:
            total = pair_add(total, scaled(0.5, c[n + 1]))
        e.append(total[0])
    cs = [a[0] for a in c]
    es = e

    def out_copy(which, to):
        return pltpu.make_async_remote_copy(
            packo.at[which, to], recvo.at[which, strip], o_ss.at[which], o_rs.at[which],
            device_id={"al": to}, device_id_type=MESH,
        )

    def combine(buf, weights, layer, tile):
        at = rows_at(tile)
        total = weights[0] * buf[0, layer, at]
        for j in range(1, len(weights)):
            total = total + weights[j] * buf[j, layer, at]
        return total

    for k in (4, 3, 5, 2, 6, 1, 7, 0):
        to = (al + k) % n_al
        for which, buf, weights in ((0, s_buf, cs), (1, u_buf, es)):
            for member in range(group):
                layer = to * group + member

                def one(tile, carry):
                    lo = combine(buf, weights, layer, tile + 1)
                    hi = combine(buf, weights, layer, tile + 1 + half_tiles)
                    packo[which, to, member, rows_at(tile)] = jnp.where(low, lo, pltpu.roll(hi, width, 1))
                    return carry

                lax.fori_loop(0, half_tiles, one, 0)
            if k:
                out_copy(which, to).start()
            else:
                pltpu.make_async_copy(packo.at[which, al], recvo.at[which, strip], lo_s.at[which]).start()

    for which, dest in ((0, xo), (1, ro)):
        many = recvo.at[which, pl.ds(0, n_al - 1)]
        pltpu.make_async_remote_copy(
            many, many, o_ss.at[which], o_rs.at[which], device_id=al_peers[0], device_id_type=MESH
        ).wait()
        pltpu.make_async_copy(packo.at[which, al], recvo.at[which, strip], lo_s.at[which]).wait()

        def one(tile, carry):
            for member in range(group):
                for tq in range(rows // LANES):
                    p = recvo[which, 2 * tq, member, rows_at(tile)]
                    r = recvo[which, 2 * tq + 1, member, rows_at(tile)]
                    dest[member, rows_at(tile), pl.ds(tq * LANES, LANES)] = jnp.where(low, p, pltpu.roll(r, width, 1))
                    dest[member, rows_at(tile + half_tiles), pl.ds(tq * LANES, LANES)] = jnp.where(
                        low, pltpu.roll(p, width, 1), r
                    )
            return carry

        lax.fori_loop(0, half_tiles, one, 0)

    for which in range(5):
        many = recv.at[which, pl.ds(0, group * (n_al - 1))]
        pltpu.make_async_remote_copy(
            many, many, t_ss.at[which], t_rs.at[which], device_id=al_peers[0], device_id_type=MESH
        ).wait_send()


def solution(mesh):
    axes = (mesh.shape["gx"], mesh.shape["gy"], mesh.shape["al"])

    def block(volt_now, volt_prev, cap_term, edge_x, edge_y, via_below, cell_ids, placed, current_table):
        group, cols, rows = volt_now.shape
        layers = group * axes[2]
        tall = cols + 2 * GHOST
        dma = pltpu.SemaphoreType.DMA
        f32 = jnp.float32
        return pl.pallas_call(
            functools.partial(kernel, axes),
            out_shape=(jax.ShapeDtypeStruct(volt_now.shape, f32),) * 2,
            in_specs=[pl.BlockSpec(memory_space=pltpu.SMEM)] + [pl.BlockSpec(memory_space=pl.ANY)] * 8,
            out_specs=(pl.BlockSpec(memory_space=pltpu.VMEM),) * 2,
            scratch_shapes=[pltpu.VMEM(volt_now.shape, f32)] * 6 + [pltpu.VMEM(cell_ids.shape, jnp.int32)] * 2 + [
                dma((8,)),
                pltpu.VMEM((5, axes[2], group, cols // 2, LANES), f32),
                pltpu.VMEM((5, layers, cols // 2, LANES), f32),
                pltpu.VMEM((8, layers, tall, LANES), f32),
                pltpu.VMEM((ITERS, layers, tall, LANES), f32),
                pltpu.VMEM((ITERS + 1, layers, tall, LANES), f32),
                pltpu.VMEM((5, 2, tall, LANES), f32),
                pltpu.VMEM((5, 2, tall, LANES), f32),
                pltpu.VMEM((cols, LANES), f32),
                pltpu.VMEM((tall, LANES), f32),
                pltpu.VMEM((2 * ITERS, TILE, LANES), f32),
                pltpu.VMEM((2, axes[0] * axes[1], LANES), f32),
                pltpu.VMEM((2, axes[2], group, cols // 2, LANES), f32),
                pltpu.VMEM((2, axes[2], group, cols // 2, LANES), f32),
                dma((5,)), dma((5,)), dma((5,)),
                dma((5, 2)), dma((5, 2)), dma((5, 2, 3)), dma((5, 2, 3)),
                dma((3,)), dma((3,)), dma((2,)), dma((2,)), dma((2,)),
            ],
            compiler_params=pltpu.CompilerParams(
                collective_id=0, has_side_effects=True, vmem_limit_bytes=60 << 20
            ),
        )(current_table, volt_now, volt_prev, cap_term, edge_x, edge_y, via_below, cell_ids, placed)

    spec = P("al", "gx", "gy")
    return jax.shard_map(
        block,
        mesh=mesh,
        in_specs=(spec,) * 6 + (P("gx", "gy"), P("gx", "gy"), P()),
        out_specs=(spec, spec),
        check_vma=False,
    )
```

```python
import functools

import jax
import jax.numpy as jnp
from jax import lax
from jax.experimental import pallas as pl
from jax.experimental.pallas import tpu as pltpu
from jax.sharding import PartitionSpec as P

ITERS = 8
MESH = pl.DeviceIdType.MESH
EX, EY, VB, WI, UP, DN, EXL, EYL = range(8)
RHS = 4
GHOST = 8
TILE = 8
LANES = 128
AT_ONCE = 5
REFINE = 3


def rows_at(tile):
    return pl.ds(pl.multiple_of(tile * TILE, TILE), TILE)


def grouped(start, stop, at_once, one):
    def turn(i, c):
        for step in range(at_once):
            one(start + i * at_once + step, c)
        return c

    lax.fori_loop(0, (stop - start) // at_once, turn, 0)


def two_sum(a, b):
    s = a + b
    t = s - a
    return s, (a - (s - t)) + (b - t)


def pair_add(a, b):
    s, t = two_sum(a[0], b[0])
    t = t + (a[1] + b[1])
    high = s + t
    return high, t - (high - s)


def pair_less(a, b):
    return pair_add(a, (-b[0], -b[1]))


def scaled(power, a):
    return power * a[0], power * a[1]


def cut(a):
    t = 4097.0 * a
    high = t - (t - a)
    return high, a - high


def pair_times(a, b):
    p = a[0] * b[0]
    (ah, al), (bh, bl) = cut(a[0]), cut(b[0])
    t = ((ah * bh - p) + ah * bl + al * bh) + al * bl
    t = t + (a[0] * b[1] + a[1] * b[0])
    high = p + t
    return high, t - (high - p)


def kernel(
    axes, table, vn_h, vp_h, cap_h, ex_h, ey_h, vb_h, ids_h, placed_h, xo, ro,
    vn, vp, cap, ex, ey, vb, ids, placed, in_s, pack, recv, coef, s_buf, u_buf, ysend, yrecv, cur, middle, part, gath, packo, recvo,
    t_ss, t_rs, l_s, x_ss, x_rs, y_ss, y_rs, r_ss, r_rs, o_ss, o_rs, lo_s,
):
    n_gx, n_gy, n_al = axes
    gx, gy, al = lax.axis_index("gx"), lax.axis_index("gy"), lax.axis_index("al")
    group, cols, rows = vn.shape
    layers = group * n_al
    width = rows // n_al
    half = cols // 2
    half_tiles = half // TILE
    own_tiles = cols // TILE
    tiles = own_tiles + 2
    odd = gy % 2
    strip = al * (1 - odd) + (n_al - 1 - al) * odd
    turn = 1 - 2 * odd

    def home(j):
        return j * (1 - odd) + (n_al - 1 - j) * odd

    at_hi = strip // (n_al - 1)
    at_lo = (n_al - 1 - strip) // (n_al - 1)
    right = {"gy": (gy + at_hi) % n_gy, "al": al + turn * (1 - at_hi)}
    left = {"gy": (gy + (n_gy - 1) * at_lo) % n_gy, "al": al - turn * (1 - at_lo)}
    fore = {"gx": (gx + 1) % n_gx}
    back = {"gx": (gx + n_gx - 1) % n_gx}
    al_peers = [{"al": (al + k) % n_al} for k in (4, 3, 5, 2, 6, 1, 7)]
    plane_peers = [
        {"gx": (gx + i) % n_gx, "gy": (gy + j) % n_gy}
        for i in (4, 5, 3, 2, 6, 7, 1, 0) for j in (2, 1, 3, 0) if i or j
    ]
    sum_groups = (plane_peers, al_peers)
    everyone = al_peers + plane_peers
    diagonal = [
        {"gx": (gx + i) % n_gx, "al": (al + j) % n_al} for i in (1, n_gx - 1) for j in (1, n_al - 1)
    ]

    barrier = pltpu.get_barrier_semaphore()
    for peer in everyone + diagonal:
        pl.semaphore_signal(barrier, inc=1, device_id=peer, device_id_type=MESH)
    reads = {
        name: pltpu.make_async_copy(src, dst, in_s.at[i])
        for i, (name, src, dst) in enumerate((
            (EX, ex_h, ex), (EY, ey_h, ey), (VB, vb_h, vb), (WI, cap_h, cap),
            ("vn", vn_h, vn), ("vp", vp_h, vp), ("ids", ids_h, ids), ("placed", placed_h, placed),
        ))
    }
    for copy in reads.values():
        copy.start()

    lane = lax.broadcasted_iota(jnp.int32, (TILE, LANES), 1)
    sub = lax.broadcasted_iota(jnp.int32, (TILE, LANES), 0)
    low = lane < width
    zero = jnp.zeros((TILE, LANES), jnp.float32)

    def value(which, layer, tile, q):
        at = (layer, rows_at(tile), pl.ds(q * LANES, LANES))
        if which == EX:
            last = (gx * cols + tile * TILE + sub) == n_gx * cols - 1
            return jnp.where(last, 0.0, ex[at])
        if which == EY:
            last = (gy * rows + q * LANES + lane) == n_gy * rows - 1
            return jnp.where(last, 0.0, ey[at])
        if which == VB:
            return jnp.where(al * group + layer == 0, 0.0, vb[at])
        if which == WI:
            return cap[at]
        return cap[at] * (4.0 * vn[at] - vp[at]) / 3.0

    def pack_array(which):
        for layer in range(group):
            def one(tile, c):
                for q in range(rows // LANES):
                    lo = value(which, layer, tile, q)
                    hi = value(which, layer, tile + half_tiles, q)
                    pack[which, 2 * q, layer, rows_at(tile)] = jnp.where(low, lo, pltpu.roll(hi, width, 1))
                    pack[which, 2 * q + 1, layer, rows_at(tile)] = jnp.where(low, pltpu.roll(lo, width, 1), hi)
                return c

            lax.fori_loop(0, half_tiles, one, 0)

    def own_copy(which):
        return pltpu.make_async_copy(
            pack.at[which, strip], recv.at[which, pl.ds(group * al, group)], l_s.at[which]
        )

    reads[EX].wait()
    pack_array(EX)
    pl.semaphore_wait(barrier, len(everyone + diagonal))
    for which in range(5):
        if which in (EY, VB, WI):
            reads[which].wait()
        if which == RHS:
            reads["vn"].wait()
            reads["vp"].wait()
        if which != EX:
            pack_array(which)
        for k in (4, 3, 5, 2, 6, 1, 7):
            to = (al + k) % n_al
            pltpu.make_async_remote_copy(
                src_ref=pack.at[which, home(to)],
                dst_ref=recv.at[which, pl.ds(group * al, group)],
                send_sem=t_ss.at[which],
                recv_sem=t_rs.at[which],
                device_id={"al": to},
                device_id_type=MESH,
            ).start()
        own_copy(which).start()

    def wait_array(which):
        many = recv.at[which, pl.ds(0, group * (n_al - 1))]
        pltpu.make_async_remote_copy(
            many, many, t_ss.at[which], t_rs.at[which], device_id={"al": al_peers[0]["al"]}, device_id_type=MESH
        ).wait_recv()
        own_copy(which).wait()

    mine = ids.at[:, pl.ds(pl.multiple_of((strip // 2) * LANES, LANES), LANES)]
    mine_placed = placed.at[:, pl.ds(pl.multiple_of((strip // 2) * LANES, LANES), LANES)]

    def stamp(tile, c):
        code = mine[rows_at(tile)]
        total = zero
        for kind in range(table.shape[0]):
            total = jnp.where(code == kind, table[kind], total)
        total = total * mine_placed[rows_at(tile)].astype(jnp.float32)
        total = jnp.where(strip % 2 == 0, total, pltpu.roll(total, width, 1))
        cur[rows_at(tile)] = jnp.where(low, total, 0.0)
        return c

    reads["ids"].wait()
    reads["placed"].wait()
    lax.fori_loop(0, own_tiles, stamp, 0)

    def unpack(which, dest):
        def one(tile, c):
            for layer in range(layers):
                v = recv[which, layer, rows_at(tile)]
                lo = jnp.where(low, v, 0.0)
                hi = jnp.where(low, pltpu.roll(v, width, 1), 0.0)
                if which == RHS and layer == 0:
                    lo = lo + cur[rows_at(tile)]
                    hi = hi + cur[rows_at(tile + half_tiles)]
                dest[layer, rows_at(tile + 1)] = lo
                dest[layer, rows_at(tile + 1 + half_tiles)] = hi
            return c

        grouped(0, half_tiles, 2, one)

    def x_copies(which, dest):
        down = pltpu.make_async_remote_copy(
            dest.at[:, pl.ds(cols, GHOST)], dest.at[:, pl.ds(0, GHOST)],
            x_ss.at[which, 0], x_rs.at[which, 0], device_id=fore, device_id_type=MESH,
        )
        up = pltpu.make_async_remote_copy(
            dest.at[:, pl.ds(GHOST, GHOST)], dest.at[:, pl.ds(GHOST + cols, GHOST)],
            x_ss.at[which, 1], x_rs.at[which, 1], device_id=back, device_id_type=MESH,
        )
        return down, up

    def y_copies(which):
        out = []
        for way, peer in ((0, right), (1, left)):
            for part_of, across, src, dst in (
                (0, {}, pl.ds(GHOST, cols), pl.ds(GHOST, cols)),
                (1, fore, pl.ds(cols, GHOST), pl.ds(0, GHOST)),
                (2, back, pl.ds(GHOST, GHOST), pl.ds(GHOST + cols, GHOST)),
            ):
                out.append(
                    pltpu.make_async_remote_copy(
                        ysend.at[which, way, src], yrecv.at[which, way, dst],
                        y_ss.at[which, way, part_of], y_rs.at[which, way, part_of],
                        device_id={**peer, **across}, device_id_type=MESH,
                    )
                )
        return out

    def start_edges(which, dest):
        for copy in x_copies(which, dest):
            copy.start()

        def one(tile, c):
            to_right, to_left = zero, zero
            for layer in range(layers):
                here = lane // GHOST == layer
                v = dest[layer, rows_at(tile)]
                to_right = jnp.where(here, pltpu.roll(v, (GHOST * layer - (width - GHOST)) % LANES, 1), to_right)
                to_left = jnp.where(here, pltpu.roll(v, GHOST * layer, 1), to_left)
            ysend[which, 0, rows_at(tile)] = to_right
            ysend[which, 1, rows_at(tile)] = to_left
            return c

        grouped(1, own_tiles + 1, 4, one)
        for copy in y_copies(which):
            copy.start()

    first = gy * n_al + strip == 0
    final = gy * n_al + strip == n_gy * n_al - 1

    def finish_edges(which, dest):
        for copy in x_copies(which, dest):
            copy.wait()
        for copy in y_copies(which):
            copy.wait()

        def one(tile, c):
            outside = jnp.logical_or(
                jnp.logical_and(gx == 0, tile == 0), jnp.logical_and(gx == n_gx - 1, tile == tiles - 1)
            )
            from_left = jnp.where(first, 0.0, yrecv[which, 0, rows_at(tile)])
            from_right = jnp.where(final, 0.0, yrecv[which, 1, rows_at(tile)])
            for layer in range(layers):
                v = dest[layer, rows_at(tile)]
                lft = pltpu.roll(from_left, (LANES - GHOST - GHOST * layer) % LANES, 1)
                rgt = pltpu.roll(from_right, (width - GHOST * layer) % LANES, 1)
                edge = jnp.where(lane < width + GHOST, rgt, jnp.where(lane >= LANES - GHOST, lft, 0.0))
                dest[layer, rows_at(tile)] = jnp.where(outside, 0.0, jnp.where(low, v, edge))
            return c

        grouped(0, tiles, 5, one)

    def before(v, previous):
        return pltpu.roll(jnp.where(sub == TILE - 1, previous, v), 1, 0)

    def after(v, following):
        return pltpu.roll(jnp.where(sub == 0, following, v), TILE - 1, 0)

    u0 = u_buf.at[0]
    c_of = [coef.at[i] for i in range(8)]

    for which in (EX, EY, VB):
        wait_array(which)
        unpack(which, c_of[which])
        start_edges(which, c_of[which])
    wait_array(WI)

    def sums_at_home(tile, c):
        at = rows_at(tile + 1)
        above = rows_at(jnp.maximum(tile, 1))
        upper = tile // half_tiles
        inner = jnp.logical_or(tile > 0, sub > 0)
        for layer in range(layers):
            held = recv[WI, layer, rows_at(tile % half_tiles)]
            held = jnp.where(upper == 0, held, pltpu.roll(held, width, 1))
            x, y = coef[EX, layer, at], coef[EY, layer, at]
            held = held + (x + jnp.where(inner, before(x, coef[EX, layer, above]), 0.0)) + (y + pltpu.roll(y, 1, 1))
            coef[WI, layer, at] = jnp.where(low, held, 0.0)
        return c

    lax.fori_loop(0, own_tiles, sums_at_home, 0)
    start_edges(WI, c_of[WI])
    wait_array(RHS)
    unpack(RHS, u0)
    start_edges(RHS, u0)
    finish_edges(EX, c_of[EX])
    finish_edges(EY, c_of[EY])

    def lefts(tile, c):
        above = jnp.maximum(tile - 1, 0)
        for layer in range(layers):
            coef[EXL, layer, rows_at(tile)] = before(coef[EX, layer, rows_at(tile)], coef[EX, layer, rows_at(above)])
            coef[EYL, layer, rows_at(tile)] = pltpu.roll(coef[EY, layer, rows_at(tile)], 1, 1)
        return c

    grouped(0, tiles, 5, lefts)
    finish_edges(VB, c_of[VB])
    finish_edges(WI, c_of[WI])

    def pivots(turn_at, c):
        each = [turn_at * AT_ONCE + step for step in range(AT_ONCE)]
        mid = layers // 2
        met = {}
        for step, tile in enumerate(each):
            at = rows_at(tile)
            seam = jnp.logical_and(sub == 0, jnp.logical_or(tile == 1, tile == tiles - 1))
            edge = jnp.logical_or(lane == 0, lane == width)
            for rank in range(mid):
                for layer, previous in ((rank, rank - 1), (layers - 1 - rank, layers - rank)):
                    held = coef[WI, layer, at]
                    below = coef[VB, layer, at]
                    over = coef[VB, layer + 1, at] if layer + 1 < layers else zero
                    diag = held + jnp.where(seam, coef[EXL, layer, at], 0.0)
                    diag = diag + jnp.where(edge, coef[EYL, layer, at], 0.0)
                    diag = diag + (below + over)
                    if rank:
                        link = below if previous < layer else over
                        diag = diag - link * (link * met[step, previous])
                    inverse = jnp.where(held > 0.0, 1.0 / diag, 0.0)
                    met[step, layer] = inverse
                    coef[WI, layer, at] = inverse
                    coef[UP, layer, at] = below * inverse
                    coef[DN, layer, at] = over * inverse
            link = coef[VB, mid, at]
            middle[at] = 1.0 / (1.0 - (link * met[step, mid - 1]) * (link * met[step, mid]))
        return c

    lax.fori_loop(0, tiles // AT_ONCE, pivots, 0)
    finish_edges(RHS, u0)

    def solve(us, at):
        mid = layers // 2
        kept = [us[layer] * coef[WI, layer, at] for layer in range(layers)]
        for rank in range(1, mid):
            lo, hi = rank, layers - 1 - rank
            kept[lo] = kept[lo] + coef[UP, lo, at] * kept[lo - 1]
            kept[hi] = kept[hi] + coef[DN, hi, at] * kept[hi + 1]
        kept[mid - 1] = middle[at] * (kept[mid - 1] + coef[DN, mid - 1, at] * kept[mid])
        kept[mid] = kept[mid] + coef[UP, mid, at] * kept[mid - 1]
        for rank in range(mid - 2, -1, -1):
            lo, hi = rank, layers - 1 - rank
            kept[lo] = kept[lo] + coef[DN, lo, at] * kept[lo + 1]
            kept[hi] = kept[hi] + coef[UP, hi, at] * kept[hi - 1]
        return kept

    def is_own(tile):
        return jnp.logical_and(tile >= 1, tile <= own_tiles)

    def begin(turn_at, acc):
        for step in range(AT_ONCE):
            tile = turn_at * AT_ONCE + step
            at = rows_at(tile)
            us = [u_buf[0, layer, at] for layer in range(layers)]
            ss = solve(us, at)
            total = zero
            for layer in range(layers):
                s_buf[0, layer, at] = ss[layer]
                total = total + ss[layer] * us[layer]
            acc = acc + jnp.where(is_own(tile), total, 0.0)
        return acc

    part[0] = lax.fori_loop(0, tiles // AT_ONCE, begin, zero)

    def apply(k, onward):
        at_once = 10 if onward else 8
        twice = jnp.where(k == 0, 1.0, 2.0)
        once = jnp.where(k == 0, 0.0, 1.0)
        older = jnp.maximum(k - 1, 0)

        def one(turn_at, accs):
            base = turn_at * at_once + (0 if onward else 1)
            ats = [rows_at(base + step) for step in range(at_once)]
            above = rows_at(jnp.maximum(base - 1, 0))
            under = rows_at(jnp.minimum(base + at_once, tiles - 1))
            cross = [zero] * at_once
            square = [zero] * at_once
            us = [[] for _ in ats]
            for layer in range(layers):
                vs = [s_buf[k, layer, at] for at in [above] + ats + [under]]
                for step, at in enumerate(ats):
                    v = vs[step + 1]
                    t = coef[EX, layer, at] * after(v, vs[step + 2]) + coef[EXL, layer, at] * before(v, vs[step])
                    t = t + (
                        coef[EY, layer, at] * pltpu.roll(v, LANES - 1, 1) + coef[EYL, layer, at] * pltpu.roll(v, 1, 1)
                    )
                    u = twice * t - once * u_buf[older, layer, at]
                    u_buf[k + 1, layer, at] = u
                    cross[step] = cross[step] + v * u
                    us[step].append(u)
            if onward:
                for step, at in enumerate(ats):
                    ss = solve(us[step], at)
                    for layer in range(layers):
                        s_buf[k + 1, layer, at] = ss[layer]
                        square[step] = square[step] + ss[layer] * us[step][layer]
            first_sum, second_sum = accs
            for step in range(at_once):
                own = is_own(base + step)
                first_sum = first_sum + jnp.where(own, cross[step], 0.0)
                second_sum = second_sum + jnp.where(own, square[step], 0.0)
            return first_sum, second_sum

        cross, square = lax.fori_loop(0, (tiles if onward else own_tiles) // at_once, one, (zero, zero))
        part[2 * k + 1] = cross
        if onward:
            part[2 * k + 2] = square

    def steps(k, c):
        apply(k, True)
        return c

    lax.fori_loop(0, ITERS - 1, steps, 0)
    apply(ITERS - 1, False)

    n_sums = 2 * ITERS
    rowed = lax.broadcasted_iota(jnp.int32, (n_sums, LANES), 0)
    laned = lax.broadcasted_iota(jnp.int32, (n_sums, LANES), 1)

    def halved(high, low_part, axis):
        while high.shape[axis] > 1:
            n = high.shape[axis] // 2
            a = lax.slice_in_dim(high, 0, n, axis=axis), lax.slice_in_dim(low_part, 0, n, axis=axis)
            b = lax.slice_in_dim(high, n, 2 * n, axis=axis), lax.slice_in_dim(low_part, n, 2 * n, axis=axis)
            high, low_part = pair_add(a, b)
        return high, low_part

    def turned(high, low_part, length, axis):
        shift = length // 2
        while shift:
            high, low_part = pair_add(
                (high, low_part), (pltpu.roll(high, shift, axis), pltpu.roll(low_part, shift, axis))
            )
            shift //= 2
        return high, low_part

    total = halved(*[jnp.where(low[None], part[...], 0.0), jnp.zeros_like(part)], 1)
    total = turned(total[0][:, 0], total[1][:, 0], LANES, 1)
    here = laned == rowed
    line = jnp.sum(jnp.where(here, total[0], 0.0), axis=0, keepdims=True) + jnp.sum(
        jnp.where(laned == rowed + LANES // 2, total[1], 0.0), axis=0, keepdims=True
    )
    for stage, peers in enumerate(sum_groups):
        count = len(peers) + 1
        gath[stage, pl.ds(count - 1, 1)] = line
        for slot, peer in enumerate(peers):
            pltpu.make_async_remote_copy(
                gath.at[stage, pl.ds(count - 1, 1)], gath.at[stage, pl.ds(slot, 1)], r_ss.at[stage], r_rs.at[stage],
                device_id=peer, device_id_type=MESH,
            ).start()
        many = gath.at[stage, pl.ds(0, count - 1)]
        pltpu.make_async_remote_copy(
            many, many, r_ss.at[stage], r_rs.at[stage], device_id=peers[0], device_id_type=MESH
        ).wait()
        got = gath[stage, 0:count]
        got_low = pltpu.roll(got, LANES // 2, 1)
        high, low_part = got[0:TILE], got_low[0:TILE]
        for i in range(1, count // TILE):
            high, low_part = pair_add(
                (high, low_part), (got[i * TILE : (i + 1) * TILE], got_low[i * TILE : (i + 1) * TILE])
            )
        high, low_part = turned(high, low_part, TILE, 0)
        line = jnp.where(low, high, pltpu.roll(low_part, LANES // 2, 1))[0:1]
    spread = jnp.broadcast_to(line, (n_sums, LANES))
    highs = jnp.broadcast_to(jnp.sum(jnp.where(here, spread, 0.0), axis=1, keepdims=True), (n_sums, LANES))
    lows = jnp.broadcast_to(
        jnp.sum(jnp.where(laned == rowed + LANES // 2, spread, 0.0), axis=1, keepdims=True), (n_sums, LANES)
    )

    def splat(array, i):
        return jnp.broadcast_to(array[i : i + 1], (TILE, LANES))

    pair = [(splat(highs, i), splat(lows, i)) for i in range(n_sums)]
    moment = [pair[0], pair[1]]
    for i in range(2, n_sums):
        moment.append(pair_less(scaled(2.0, pair[i]), pair[i % 2]))
    q = [pair_less(moment[0], moment[1])]
    for i in range(1, n_sums - 1):
        q.append(pair_less(moment[i], scaled(0.5, pair_add(moment[i + 1], moment[i - 1]))))

    def stacked(parts):
        out = parts[0]
        for i in range(1, ITERS):
            out = jnp.where(sub == i, parts[i], out)
        return out

    def column(j, which):
        return stacked([q[i + j][which] for i in range(ITERS)]), stacked([q[abs(i - j)][which] for i in range(ITERS)])

    mat = []
    for j in range(ITERS):
        (high_a, high_b), (low_a, low_b) = column(j, 0), column(j, 1)
        mat.append(scaled(0.5, pair_add((high_a, low_a), (high_b, low_b))))
    vec = (stacked([moment[i][0] for i in range(ITERS)]), stacked([moment[i][1] for i in range(ITERS)]))

    left_over = [m[0] for m in mat]
    lower, inv = [], []
    for k in range(ITERS):
        inv.append(1.0 / splat(left_over[k], k))
        lower.append(jnp.where(sub > k, left_over[k] * inv[k], 0.0))
        for j in range(k + 1, ITERS):
            left_over[j] = left_over[j] - lower[k] * splat(left_over[j], k)

    def solved(right_side):
        for k in range(ITERS - 1):
            right_side = right_side - lower[k] * splat(right_side, k)
        out = [None] * ITERS
        for k in range(ITERS - 1, -1, -1):
            out[k] = splat(right_side, k) * inv[k]
            right_side = right_side - jnp.where(sub < k, left_over[k], 0.0) * out[k]
        return out

    c = [(a, zero) for a in solved(vec[0])]
    for _ in range(REFINE):
        rest = vec
        for j in range(ITERS):
            rest = pair_less(rest, pair_times(mat[j], c[j]))
        c = [pair_add(a, (b, zero)) for a, b in zip(c, solved(rest[0]))]
    e = []
    for n in range(ITERS + 1):
        total = (jnp.ones_like(zero), zero) if n == 0 else (zero, zero)
        if n < ITERS:
            total = pair_less(total, c[n])
        if n >= 1:
            total = pair_add(total, c[0] if n == 1 else scaled(0.5, c[n - 1]))
        if n + 1 < ITERS:
            total = pair_add(total, scaled(0.5, c[n + 1]))
        e.append(total[0])
    cs = [a[0] for a in c]
    es = e

    def out_copy(which, to):
        return pltpu.make_async_remote_copy(
            packo.at[which, to], recvo.at[which, strip], o_ss.at[which], o_rs.at[which],
            device_id={"al": to}, device_id_type=MESH,
        )

    def combine(buf, weights, layer, tile):
        at = rows_at(tile)
        total = weights[0] * buf[0, layer, at]
        for j in range(1, len(weights)):
            total = total + weights[j] * buf[j, layer, at]
        return total

    for k in (4, 3, 5, 2, 6, 1, 7, 0):
        to = (al + k) % n_al
        for which, buf, weights in ((0, s_buf, cs), (1, u_buf, es)):
            for member in range(group):
                layer = to * group + member

                def one(tile, carry):
                    lo = combine(buf, weights, layer, tile + 1)
                    hi = combine(buf, weights, layer, tile + 1 + half_tiles)
                    packo[which, to, member, rows_at(tile)] = jnp.where(low, lo, pltpu.roll(hi, width, 1))
                    return carry

                grouped(0, half_tiles, half_tiles, one)
            if k:
                out_copy(which, to).start()
            else:
                pltpu.make_async_copy(packo.at[which, al], recvo.at[which, strip], lo_s.at[which]).start()

    for which, dest in ((0, xo), (1, ro)):
        many = recvo.at[which, pl.ds(0, n_al - 1)]
        pltpu.make_async_remote_copy(
            many, many, o_ss.at[which], o_rs.at[which], device_id=al_peers[0], device_id_type=MESH
        ).wait()
        pltpu.make_async_copy(packo.at[which, al], recvo.at[which, strip], lo_s.at[which]).wait()

        def one(tile, carry):
            for member in range(group):
                for tq in range(rows // LANES):
                    p = recvo[which, 2 * tq, member, rows_at(tile)]
                    r = recvo[which, 2 * tq + 1, member, rows_at(tile)]
                    dest[member, rows_at(tile), pl.ds(tq * LANES, LANES)] = jnp.where(low, p, pltpu.roll(r, width, 1))
                    dest[member, rows_at(tile + half_tiles), pl.ds(tq * LANES, LANES)] = jnp.where(
                        low, pltpu.roll(p, width, 1), r
                    )
            return carry

        lax.fori_loop(0, half_tiles, one, 0)

    for which in range(5):
        many = recv.at[which, pl.ds(0, group * (n_al - 1))]
        pltpu.make_async_remote_copy(
            many, many, t_ss.at[which], t_rs.at[which], device_id=al_peers[0], device_id_type=MESH
        ).wait_send()


def solution(mesh):
    axes = (mesh.shape["gx"], mesh.shape["gy"], mesh.shape["al"])

    def block(volt_now, volt_prev, cap_term, edge_x, edge_y, via_below, cell_ids, placed, current_table):
        group, cols, rows = volt_now.shape
        layers = group * axes[2]
        tall = cols + 2 * GHOST
        dma = pltpu.SemaphoreType.DMA
        f32 = jnp.float32
        return pl.pallas_call(
            functools.partial(kernel, axes),
            out_shape=(jax.ShapeDtypeStruct(volt_now.shape, f32),) * 2,
            in_specs=[pl.BlockSpec(memory_space=pltpu.SMEM)] + [pl.BlockSpec(memory_space=pl.ANY)] * 8,
            out_specs=(pl.BlockSpec(memory_space=pltpu.VMEM),) * 2,
            scratch_shapes=[pltpu.VMEM(volt_now.shape, f32)] * 6 + [pltpu.VMEM(cell_ids.shape, jnp.int32)] * 2 + [
                dma((8,)),
                pltpu.VMEM((5, axes[2], group, cols // 2, LANES), f32),
                pltpu.VMEM((5, layers, cols // 2, LANES), f32),
                pltpu.VMEM((8, layers, tall, LANES), f32),
                pltpu.VMEM((ITERS, layers, tall, LANES), f32),
                pltpu.VMEM((ITERS + 1, layers, tall, LANES), f32),
                pltpu.VMEM((5, 2, tall, LANES), f32),
                pltpu.VMEM((5, 2, tall, LANES), f32),
                pltpu.VMEM((cols, LANES), f32),
                pltpu.VMEM((tall, LANES), f32),
                pltpu.VMEM((2 * ITERS, TILE, LANES), f32),
                pltpu.VMEM((2, axes[0] * axes[1], LANES), f32),
                pltpu.VMEM((2, axes[2], group, cols // 2, LANES), f32),
                pltpu.VMEM((2, axes[2], group, cols // 2, LANES), f32),
                dma((5,)), dma((5,)), dma((5,)),
                dma((5, 2)), dma((5, 2)), dma((5, 2, 3)), dma((5, 2, 3)),
                dma((3,)), dma((3,)), dma((2,)), dma((2,)), dma((2,)),
            ],
            compiler_params=pltpu.CompilerParams(
                collective_id=0, has_side_effects=True, vmem_limit_bytes=60 << 20
            ),
        )(current_table, volt_now, volt_prev, cap_term, edge_x, edge_y, via_below, cell_ids, placed)

    spec = P("al", "gx", "gy")
    return jax.shard_map(
        block,
        mesh=mesh,
        in_specs=(spec,) * 6 + (P("gx", "gy"), P("gx", "gy"), P()),
        out_specs=(spec, spec),
        check_vma=False,
    )
```

```python
import functools

import jax
import jax.numpy as jnp
from jax import lax
from jax.experimental import pallas as pl
from jax.experimental.pallas import tpu as pltpu
from jax.sharding import PartitionSpec as P

ITERS = 8
MESH = pl.DeviceIdType.MESH
EX, EY, VB, WI, UP, DN, EXL, EYL = range(8)
RHS = 4
GHOST = 8
TILE = 8
LANES = 128
AT_ONCE = 5
REFINE = 3


def rows_at(tile):
    return pl.ds(pl.multiple_of(tile * TILE, TILE), TILE)


def grouped(start, stop, at_once, one):
    def turn(i, c):
        for step in range(at_once):
            one(start + i * at_once + step, c)
        return c

    lax.fori_loop(0, (stop - start) // at_once, turn, 0)


def two_sum(a, b):
    s = a + b
    t = s - a
    return s, (a - (s - t)) + (b - t)


def pair_add(a, b):
    s, t = two_sum(a[0], b[0])
    t = t + (a[1] + b[1])
    high = s + t
    return high, t - (high - s)


def pair_less(a, b):
    return pair_add(a, (-b[0], -b[1]))


def scaled(power, a):
    return power * a[0], power * a[1]


def cut(a):
    t = 4097.0 * a
    high = t - (t - a)
    return high, a - high


def pair_times(a, b):
    p = a[0] * b[0]
    (ah, al), (bh, bl) = cut(a[0]), cut(b[0])
    t = ((ah * bh - p) + ah * bl + al * bh) + al * bl
    t = t + (a[0] * b[1] + a[1] * b[0])
    high = p + t
    return high, t - (high - p)


def kernel(
    axes, table, vn_h, vp_h, cap_h, ex_h, ey_h, vb_h, ids_h, placed_h, xo, ro,
    vn, vp, cap, ex, ey, vb, ids, placed, in_s, pack, recv, coef, s_buf, u_buf, ysend, yrecv, cur, middle, part, gath, packo, recvo,
    t_ss, t_rs, l_s, x_ss, x_rs, y_ss, y_rs, r_ss, r_rs, o_ss, o_rs, lo_s,
):
    n_gx, n_gy, n_al = axes
    gx, gy, al = lax.axis_index("gx"), lax.axis_index("gy"), lax.axis_index("al")
    group, cols, rows = vn.shape
    layers = group * n_al
    width = rows // n_al
    half = cols // 2
    half_tiles = half // TILE
    own_tiles = cols // TILE
    tiles = own_tiles + 2
    odd = gy % 2
    strip = al * (1 - odd) + (n_al - 1 - al) * odd
    turn = 1 - 2 * odd

    def home(j):
        return j * (1 - odd) + (n_al - 1 - j) * odd

    at_hi = strip // (n_al - 1)
    at_lo = (n_al - 1 - strip) // (n_al - 1)
    right = {"gy": (gy + at_hi) % n_gy, "al": al + turn * (1 - at_hi)}
    left = {"gy": (gy + (n_gy - 1) * at_lo) % n_gy, "al": al - turn * (1 - at_lo)}
    fore = {"gx": (gx + 1) % n_gx}
    back = {"gx": (gx + n_gx - 1) % n_gx}
    al_peers = [{"al": (al + k) % n_al} for k in (4, 3, 5, 2, 6, 1, 7)]
    plane_peers = [
        {"gx": (gx + i) % n_gx, "gy": (gy + j) % n_gy}
        for i in (4, 5, 3, 2, 6, 7, 1, 0) for j in (2, 1, 3, 0) if i or j
    ]
    sum_groups = (plane_peers, al_peers)
    everyone = al_peers + plane_peers
    diagonal = [
        {"gx": (gx + i) % n_gx, "al": (al + j) % n_al} for i in (1, n_gx - 1) for j in (1, n_al - 1)
    ]

    barrier = pltpu.get_barrier_semaphore()
    for peer in everyone + diagonal:
        pl.semaphore_signal(barrier, inc=1, device_id=peer, device_id_type=MESH)
    reads = {
        name: pltpu.make_async_copy(src, dst, in_s.at[i])
        for i, (name, src, dst) in enumerate((
            (EX, ex_h, ex), (EY, ey_h, ey), (VB, vb_h, vb), (WI, cap_h, cap),
            ("vn", vn_h, vn), ("vp", vp_h, vp), ("ids", ids_h, ids), ("placed", placed_h, placed),
        ))
    }
    for copy in reads.values():
        copy.start()

    lane = lax.broadcasted_iota(jnp.int32, (TILE, LANES), 1)
    sub = lax.broadcasted_iota(jnp.int32, (TILE, LANES), 0)
    low = lane < width
    zero = jnp.zeros((TILE, LANES), jnp.float32)

    def value(which, layer, tile, q):
        at = (layer, rows_at(tile), pl.ds(q * LANES, LANES))
        if which == EX:
            last = (gx * cols + tile * TILE + sub) == n_gx * cols - 1
            return jnp.where(last, 0.0, ex[at])
        if which == EY:
            last = (gy * rows + q * LANES + lane) == n_gy * rows - 1
            return jnp.where(last, 0.0, ey[at])
        if which == VB:
            return jnp.where(al * group + layer == 0, 0.0, vb[at])
        if which == WI:
            return cap[at]
        return cap[at] * (4.0 * vn[at] - vp[at]) / 3.0

    def pack_array(which):
        for layer in range(group):
            def one(tile, c):
                for q in range(rows // LANES):
                    lo = value(which, layer, tile, q)
                    hi = value(which, layer, tile + half_tiles, q)
                    pack[which, 2 * q, layer, rows_at(tile)] = jnp.where(low, lo, pltpu.roll(hi, width, 1))
                    pack[which, 2 * q + 1, layer, rows_at(tile)] = jnp.where(low, pltpu.roll(lo, width, 1), hi)
                return c

            lax.fori_loop(0, half_tiles, one, 0)

    def own_copy(which):
        return pltpu.make_async_copy(
            pack.at[which, strip], recv.at[which, pl.ds(group * al, group)], l_s.at[which]
        )

    reads[EX].wait()
    pack_array(EX)
    pl.semaphore_wait(barrier, len(everyone + diagonal))
    for which in range(5):
        if which in (EY, VB, WI):
            reads[which].wait()
        if which == RHS:
            reads["vn"].wait()
            reads["vp"].wait()
        if which != EX:
            pack_array(which)
        for k in (4, 3, 5, 2, 6, 1, 7):
            to = (al + k) % n_al
            pltpu.make_async_remote_copy(
                src_ref=pack.at[which, home(to)],
                dst_ref=recv.at[which, pl.ds(group * al, group)],
                send_sem=t_ss.at[which],
                recv_sem=t_rs.at[which],
                device_id={"al": to},
                device_id_type=MESH,
            ).start()
        own_copy(which).start()

    def wait_array(which):
        many = recv.at[which, pl.ds(0, group * (n_al - 1))]
        pltpu.make_async_remote_copy(
            many, many, t_ss.at[which], t_rs.at[which], device_id={"al": al_peers[0]["al"]}, device_id_type=MESH
        ).wait_recv()
        own_copy(which).wait()

    mine = ids.at[:, pl.ds(pl.multiple_of((strip // 2) * LANES, LANES), LANES)]
    mine_placed = placed.at[:, pl.ds(pl.multiple_of((strip // 2) * LANES, LANES), LANES)]

    def stamp(tile, c):
        code = mine[rows_at(tile)]
        total = zero
        for kind in range(table.shape[0]):
            total = jnp.where(code == kind, table[kind], total)
        total = total * mine_placed[rows_at(tile)].astype(jnp.float32)
        total = jnp.where(strip % 2 == 0, total, pltpu.roll(total, width, 1))
        cur[rows_at(tile)] = jnp.where(low, total, 0.0)
        return c

    reads["ids"].wait()
    reads["placed"].wait()
    lax.fori_loop(0, own_tiles, stamp, 0)

    def unpack(which, dest):
        def one(tile, c):
            for layer in range(layers):
                v = recv[which, layer, rows_at(tile)]
                lo = jnp.where(low, v, 0.0)
                hi = jnp.where(low, pltpu.roll(v, width, 1), 0.0)
                if which == RHS and layer == 0:
                    lo = lo + cur[rows_at(tile)]
                    hi = hi + cur[rows_at(tile + half_tiles)]
                dest[layer, rows_at(tile + 1)] = lo
                dest[layer, rows_at(tile + 1 + half_tiles)] = hi
            return c

        grouped(0, half_tiles, half_tiles, one)

    def x_copies(which, dest):
        down = pltpu.make_async_remote_copy(
            dest.at[:, pl.ds(cols, GHOST)], dest.at[:, pl.ds(0, GHOST)],
            x_ss.at[which, 0], x_rs.at[which, 0], device_id=fore, device_id_type=MESH,
        )
        up = pltpu.make_async_remote_copy(
            dest.at[:, pl.ds(GHOST, GHOST)], dest.at[:, pl.ds(GHOST + cols, GHOST)],
            x_ss.at[which, 1], x_rs.at[which, 1], device_id=back, device_id_type=MESH,
        )
        return down, up

    def y_copies(which):
        out = []
        for way, peer in ((0, right), (1, left)):
            for part_of, across, src, dst in (
                (0, {}, pl.ds(GHOST, cols), pl.ds(GHOST, cols)),
                (1, fore, pl.ds(cols, GHOST), pl.ds(0, GHOST)),
                (2, back, pl.ds(GHOST, GHOST), pl.ds(GHOST + cols, GHOST)),
            ):
                out.append(
                    pltpu.make_async_remote_copy(
                        ysend.at[which, way, src], yrecv.at[which, way, dst],
                        y_ss.at[which, way, part_of], y_rs.at[which, way, part_of],
                        device_id={**peer, **across}, device_id_type=MESH,
                    )
                )
        return out

    def start_edges(which, dest):
        for copy in x_copies(which, dest):
            copy.start()

        def one(tile, c):
            to_right, to_left = zero, zero
            for layer in range(layers):
                here = lane // GHOST == layer
                v = dest[layer, rows_at(tile)]
                to_right = jnp.where(here, pltpu.roll(v, (GHOST * layer - (width - GHOST)) % LANES, 1), to_right)
                to_left = jnp.where(here, pltpu.roll(v, GHOST * layer, 1), to_left)
            ysend[which, 0, rows_at(tile)] = to_right
            ysend[which, 1, rows_at(tile)] = to_left
            return c

        grouped(1, own_tiles + 1, 4, one)
        for copy in y_copies(which):
            copy.start()

    first = gy * n_al + strip == 0
    final = gy * n_al + strip == n_gy * n_al - 1

    def finish_edges(which, dest):
        for copy in x_copies(which, dest):
            copy.wait()
        for copy in y_copies(which):
            copy.wait()

        def one(tile, c):
            outside = jnp.logical_or(
                jnp.logical_and(gx == 0, tile == 0), jnp.logical_and(gx == n_gx - 1, tile == tiles - 1)
            )
            from_left = jnp.where(first, 0.0, yrecv[which, 0, rows_at(tile)])
            from_right = jnp.where(final, 0.0, yrecv[which, 1, rows_at(tile)])
            for layer in range(layers):
                v = dest[layer, rows_at(tile)]
                lft = pltpu.roll(from_left, (LANES - GHOST - GHOST * layer) % LANES, 1)
                rgt = pltpu.roll(from_right, (width - GHOST * layer) % LANES, 1)
                edge = jnp.where(lane < width + GHOST, rgt, jnp.where(lane >= LANES - GHOST, lft, 0.0))
                dest[layer, rows_at(tile)] = jnp.where(outside, 0.0, jnp.where(low, v, edge))
            return c

        grouped(0, tiles, 5, one)

    def before(v, previous):
        return pltpu.roll(jnp.where(sub == TILE - 1, previous, v), 1, 0)

    def after(v, following):
        return pltpu.roll(jnp.where(sub == 0, following, v), TILE - 1, 0)

    u0 = u_buf.at[0]
    c_of = [coef.at[i] for i in range(8)]

    for which in (EX, EY, VB):
        wait_array(which)
        unpack(which, c_of[which])
        start_edges(which, c_of[which])
    wait_array(WI)

    def sums_at_home(tile, c):
        at = rows_at(tile + 1)
        above = rows_at(jnp.maximum(tile, 1))
        upper = tile // half_tiles
        inner = jnp.logical_or(tile > 0, sub > 0)
        for layer in range(layers):
            held = recv[WI, layer, rows_at(tile % half_tiles)]
            held = jnp.where(upper == 0, held, pltpu.roll(held, width, 1))
            x, y = coef[EX, layer, at], coef[EY, layer, at]
            held = held + (x + jnp.where(inner, before(x, coef[EX, layer, above]), 0.0)) + (y + pltpu.roll(y, 1, 1))
            coef[WI, layer, at] = jnp.where(low, held, 0.0)
        return c

    grouped(0, own_tiles, 4, sums_at_home)
    start_edges(WI, c_of[WI])
    wait_array(RHS)
    unpack(RHS, u0)
    start_edges(RHS, u0)
    finish_edges(EX, c_of[EX])
    finish_edges(EY, c_of[EY])

    def lefts(tile, c):
        above = jnp.maximum(tile - 1, 0)
        for layer in range(layers):
            coef[EXL, layer, rows_at(tile)] = before(coef[EX, layer, rows_at(tile)], coef[EX, layer, rows_at(above)])
            coef[EYL, layer, rows_at(tile)] = pltpu.roll(coef[EY, layer, rows_at(tile)], 1, 1)
        return c

    grouped(0, tiles, 5, lefts)
    finish_edges(VB, c_of[VB])
    finish_edges(WI, c_of[WI])

    def pivots(turn_at, c):
        each = [turn_at * AT_ONCE + step for step in range(AT_ONCE)]
        mid = layers // 2
        met = {}
        for step, tile in enumerate(each):
            at = rows_at(tile)
            seam = jnp.logical_and(sub == 0, jnp.logical_or(tile == 1, tile == tiles - 1))
            edge = jnp.logical_or(lane == 0, lane == width)
            for rank in range(mid):
                for layer, previous in ((rank, rank - 1), (layers - 1 - rank, layers - rank)):
                    held = coef[WI, layer, at]
                    below = coef[VB, layer, at]
                    over = coef[VB, layer + 1, at] if layer + 1 < layers else zero
                    diag = held + jnp.where(seam, coef[EXL, layer, at], 0.0)
                    diag = diag + jnp.where(edge, coef[EYL, layer, at], 0.0)
                    diag = diag + (below + over)
                    if rank:
                        link = below if previous < layer else over
                        diag = diag - link * (link * met[step, previous])
                    inverse = jnp.where(held > 0.0, 1.0 / diag, 0.0)
                    met[step, layer] = inverse
                    coef[WI, layer, at] = inverse
                    coef[UP, layer, at] = below * inverse
                    coef[DN, layer, at] = over * inverse
            link = coef[VB, mid, at]
            middle[at] = 1.0 / (1.0 - (link * met[step, mid - 1]) * (link * met[step, mid]))
        return c

    lax.fori_loop(0, tiles // AT_ONCE, pivots, 0)
    finish_edges(RHS, u0)

    def solve(us, at):
        mid = layers // 2
        kept = [us[layer] * coef[WI, layer, at] for layer in range(layers)]
        for rank in range(1, mid):
            lo, hi = rank, layers - 1 - rank
            kept[lo] = kept[lo] + coef[UP, lo, at] * kept[lo - 1]
            kept[hi] = kept[hi] + coef[DN, hi, at] * kept[hi + 1]
        kept[mid - 1] = middle[at] * (kept[mid - 1] + coef[DN, mid - 1, at] * kept[mid])
        kept[mid] = kept[mid] + coef[UP, mid, at] * kept[mid - 1]
        for rank in range(mid - 2, -1, -1):
            lo, hi = rank, layers - 1 - rank
            kept[lo] = kept[lo] + coef[DN, lo, at] * kept[lo + 1]
            kept[hi] = kept[hi] + coef[UP, hi, at] * kept[hi - 1]
        return kept

    def is_own(tile):
        return jnp.logical_and(tile >= 1, tile <= own_tiles)

    def begin(turn_at, acc):
        for step in range(AT_ONCE):
            tile = turn_at * AT_ONCE + step
            at = rows_at(tile)
            us = [u_buf[0, layer, at] for layer in range(layers)]
            ss = solve(us, at)
            total = zero
            for layer in range(layers):
                s_buf[0, layer, at] = ss[layer]
                total = total + ss[layer] * us[layer]
            acc = acc + jnp.where(is_own(tile), total, 0.0)
        return acc

    part[0] = lax.fori_loop(0, tiles // AT_ONCE, begin, zero)

    def apply(k, onward):
        at_once = 10 if onward else 8
        twice = jnp.where(k == 0, 1.0, 2.0)
        once = jnp.where(k == 0, 0.0, 1.0)
        older = jnp.maximum(k - 1, 0)

        def one(turn_at, accs):
            base = turn_at * at_once + (0 if onward else 1)
            ats = [rows_at(base + step) for step in range(at_once)]
            above = rows_at(jnp.maximum(base - 1, 0))
            under = rows_at(jnp.minimum(base + at_once, tiles - 1))
            cross = [zero] * at_once
            square = [zero] * at_once
            us = [[] for _ in ats]
            for layer in range(layers):
                vs = [s_buf[k, layer, at] for at in [above] + ats + [under]]
                for step, at in enumerate(ats):
                    v = vs[step + 1]
                    t = coef[EX, layer, at] * after(v, vs[step + 2]) + coef[EXL, layer, at] * before(v, vs[step])
                    t = t + (
                        coef[EY, layer, at] * pltpu.roll(v, LANES - 1, 1) + coef[EYL, layer, at] * pltpu.roll(v, 1, 1)
                    )
                    u = twice * t - once * u_buf[older, layer, at]
                    u_buf[k + 1, layer, at] = u
                    cross[step] = cross[step] + v * u
                    us[step].append(u)
            if onward:
                for step, at in enumerate(ats):
                    ss = solve(us[step], at)
                    for layer in range(layers):
                        s_buf[k + 1, layer, at] = ss[layer]
                        square[step] = square[step] + ss[layer] * us[step][layer]
            first_sum, second_sum = accs
            for step in range(at_once):
                own = is_own(base + step)
                first_sum = first_sum + jnp.where(own, cross[step], 0.0)
                second_sum = second_sum + jnp.where(own, square[step], 0.0)
            return first_sum, second_sum

        cross, square = lax.fori_loop(0, (tiles if onward else own_tiles) // at_once, one, (zero, zero))
        part[2 * k + 1] = cross
        if onward:
            part[2 * k + 2] = square

    def steps(k, c):
        apply(k, True)
        return c

    lax.fori_loop(0, ITERS - 1, steps, 0)
    apply(ITERS - 1, False)

    n_sums = 2 * ITERS
    rowed = lax.broadcasted_iota(jnp.int32, (n_sums, LANES), 0)
    laned = lax.broadcasted_iota(jnp.int32, (n_sums, LANES), 1)

    def halved(high, low_part, axis):
        while high.shape[axis] > 1:
            n = high.shape[axis] // 2
            a = lax.slice_in_dim(high, 0, n, axis=axis), lax.slice_in_dim(low_part, 0, n, axis=axis)
            b = lax.slice_in_dim(high, n, 2 * n, axis=axis), lax.slice_in_dim(low_part, n, 2 * n, axis=axis)
            high, low_part = pair_add(a, b)
        return high, low_part

    def turned(high, low_part, length, axis):
        shift = length // 2
        while shift:
            high, low_part = pair_add(
                (high, low_part), (pltpu.roll(high, shift, axis), pltpu.roll(low_part, shift, axis))
            )
            shift //= 2
        return high, low_part

    total = halved(*[jnp.where(low[None], part[...], 0.0), jnp.zeros_like(part)], 1)
    total = turned(total[0][:, 0], total[1][:, 0], LANES, 1)
    here = laned == rowed
    line = jnp.sum(jnp.where(here, total[0], 0.0), axis=0, keepdims=True) + jnp.sum(
        jnp.where(laned == rowed + LANES // 2, total[1], 0.0), axis=0, keepdims=True
    )
    for stage, peers in enumerate(sum_groups):
        count = len(peers) + 1
        gath[stage, pl.ds(count - 1, 1)] = line
        for slot, peer in enumerate(peers):
            pltpu.make_async_remote_copy(
                gath.at[stage, pl.ds(count - 1, 1)], gath.at[stage, pl.ds(slot, 1)], r_ss.at[stage], r_rs.at[stage],
                device_id=peer, device_id_type=MESH,
            ).start()
        many = gath.at[stage, pl.ds(0, count - 1)]
        pltpu.make_async_remote_copy(
            many, many, r_ss.at[stage], r_rs.at[stage], device_id=peers[0], device_id_type=MESH
        ).wait()
        got = gath[stage, 0:count]
        got_low = pltpu.roll(got, LANES // 2, 1)
        high, low_part = got[0:TILE], got_low[0:TILE]
        for i in range(1, count // TILE):
            high, low_part = pair_add(
                (high, low_part), (got[i * TILE : (i + 1) * TILE], got_low[i * TILE : (i + 1) * TILE])
            )
        high, low_part = turned(high, low_part, TILE, 0)
        line = jnp.where(low, high, pltpu.roll(low_part, LANES // 2, 1))[0:1]
    spread = jnp.broadcast_to(line, (n_sums, LANES))
    highs = jnp.broadcast_to(jnp.sum(jnp.where(here, spread, 0.0), axis=1, keepdims=True), (n_sums, LANES))
    lows = jnp.broadcast_to(
        jnp.sum(jnp.where(laned == rowed + LANES // 2, spread, 0.0), axis=1, keepdims=True), (n_sums, LANES)
    )

    def splat(array, i):
        return jnp.broadcast_to(array[i : i + 1], (TILE, LANES))

    pair = [(splat(highs, i), splat(lows, i)) for i in range(n_sums)]
    moment = [pair[0], pair[1]]
    for i in range(2, n_sums):
        moment.append(pair_less(scaled(2.0, pair[i]), pair[i % 2]))
    q = [pair_less(moment[0], moment[1])]
    for i in range(1, n_sums - 1):
        q.append(pair_less(moment[i], scaled(0.5, pair_add(moment[i + 1], moment[i - 1]))))

    def stacked(parts):
        out = parts[0]
        for i in range(1, ITERS):
            out = jnp.where(sub == i, parts[i], out)
        return out

    def column(j, which):
        return stacked([q[i + j][which] for i in range(ITERS)]), stacked([q[abs(i - j)][which] for i in range(ITERS)])

    mat = []
    for j in range(ITERS):
        (high_a, high_b), (low_a, low_b) = column(j, 0), column(j, 1)
        mat.append(scaled(0.5, pair_add((high_a, low_a), (high_b, low_b))))
    vec = (stacked([moment[i][0] for i in range(ITERS)]), stacked([moment[i][1] for i in range(ITERS)]))

    left_over = [m[0] for m in mat]
    lower, inv = [], []
    for k in range(ITERS):
        inv.append(1.0 / splat(left_over[k], k))
        lower.append(jnp.where(sub > k, left_over[k] * inv[k], 0.0))
        for j in range(k + 1, ITERS):
            left_over[j] = left_over[j] - lower[k] * splat(left_over[j], k)

    def solved(right_side):
        for k in range(ITERS - 1):
            right_side = right_side - lower[k] * splat(right_side, k)
        out = [None] * ITERS
        for k in range(ITERS - 1, -1, -1):
            out[k] = splat(right_side, k) * inv[k]
            right_side = right_side - jnp.where(sub < k, left_over[k], 0.0) * out[k]
        return out

    c = [(a, zero) for a in solved(vec[0])]
    for _ in range(REFINE):
        rest = vec
        for j in range(ITERS):
            rest = pair_less(rest, pair_times(mat[j], c[j]))
        c = [pair_add(a, (b, zero)) for a, b in zip(c, solved(rest[0]))]
    e = []
    for n in range(ITERS + 1):
        total = (jnp.ones_like(zero), zero) if n == 0 else (zero, zero)
        if n < ITERS:
            total = pair_less(total, c[n])
        if n >= 1:
            total = pair_add(total, c[0] if n == 1 else scaled(0.5, c[n - 1]))
        if n + 1 < ITERS:
            total = pair_add(total, scaled(0.5, c[n + 1]))
        e.append(total[0])
    cs = [a[0] for a in c]
    es = e

    def out_copy(which, to):
        return pltpu.make_async_remote_copy(
            packo.at[which, to], recvo.at[which, strip], o_ss.at[which], o_rs.at[which],
            device_id={"al": to}, device_id_type=MESH,
        )

    def combine(buf, weights, layer, tile):
        at = rows_at(tile)
        total = weights[0] * buf[0, layer, at]
        for j in range(1, len(weights)):
            total = total + weights[j] * buf[j, layer, at]
        return total

    for k in (4, 3, 5, 2, 6, 1, 7, 0):
        to = (al + k) % n_al
        for which, buf, weights in ((0, s_buf, cs), (1, u_buf, es)):
            for member in range(group):
                layer = to * group + member

                def one(tile, carry):
                    lo = combine(buf, weights, layer, tile + 1)
                    hi = combine(buf, weights, layer, tile + 1 + half_tiles)
                    packo[which, to, member, rows_at(tile)] = jnp.where(low, lo, pltpu.roll(hi, width, 1))
                    return carry

                grouped(0, half_tiles, half_tiles, one)
            if k:
                out_copy(which, to).start()
            else:
                pltpu.make_async_copy(packo.at[which, al], recvo.at[which, strip], lo_s.at[which]).start()

    for which, dest in ((0, xo), (1, ro)):
        many = recvo.at[which, pl.ds(0, n_al - 1)]
        pltpu.make_async_remote_copy(
            many, many, o_ss.at[which], o_rs.at[which], device_id=al_peers[0], device_id_type=MESH
        ).wait()
        pltpu.make_async_copy(packo.at[which, al], recvo.at[which, strip], lo_s.at[which]).wait()

        def one(tile, carry):
            for member in range(group):
                for tq in range(rows // LANES):
                    p = recvo[which, 2 * tq, member, rows_at(tile)]
                    r = recvo[which, 2 * tq + 1, member, rows_at(tile)]
                    dest[member, rows_at(tile), pl.ds(tq * LANES, LANES)] = jnp.where(low, p, pltpu.roll(r, width, 1))
                    dest[member, rows_at(tile + half_tiles), pl.ds(tq * LANES, LANES)] = jnp.where(
                        low, pltpu.roll(p, width, 1), r
                    )
            return carry

        grouped(0, half_tiles, half_tiles, one)

    for which in range(5):
        many = recv.at[which, pl.ds(0, group * (n_al - 1))]
        pltpu.make_async_remote_copy(
            many, many, t_ss.at[which], t_rs.at[which], device_id=al_peers[0], device_id_type=MESH
        ).wait_send()


def solution(mesh):
    axes = (mesh.shape["gx"], mesh.shape["gy"], mesh.shape["al"])

    def block(volt_now, volt_prev, cap_term, edge_x, edge_y, via_below, cell_ids, placed, current_table):
        group, cols, rows = volt_now.shape
        layers = group * axes[2]
        tall = cols + 2 * GHOST
        dma = pltpu.SemaphoreType.DMA
        f32 = jnp.float32
        return pl.pallas_call(
            functools.partial(kernel, axes),
            out_shape=(jax.ShapeDtypeStruct(volt_now.shape, f32),) * 2,
            in_specs=[pl.BlockSpec(memory_space=pltpu.SMEM)] + [pl.BlockSpec(memory_space=pl.ANY)] * 8,
            out_specs=(pl.BlockSpec(memory_space=pltpu.VMEM),) * 2,
            scratch_shapes=[pltpu.VMEM(volt_now.shape, f32)] * 6 + [pltpu.VMEM(cell_ids.shape, jnp.int32)] * 2 + [
                dma((8,)),
                pltpu.VMEM((5, axes[2], group, cols // 2, LANES), f32),
                pltpu.VMEM((5, layers, cols // 2, LANES), f32),
                pltpu.VMEM((8, layers, tall, LANES), f32),
                pltpu.VMEM((ITERS, layers, tall, LANES), f32),
                pltpu.VMEM((ITERS + 1, layers, tall, LANES), f32),
                pltpu.VMEM((5, 2, tall, LANES), f32),
                pltpu.VMEM((5, 2, tall, LANES), f32),
                pltpu.VMEM((cols, LANES), f32),
                pltpu.VMEM((tall, LANES), f32),
                pltpu.VMEM((2 * ITERS, TILE, LANES), f32),
                pltpu.VMEM((2, axes[0] * axes[1], LANES), f32),
                pltpu.VMEM((2, axes[2], group, cols // 2, LANES), f32),
                pltpu.VMEM((2, axes[2], group, cols // 2, LANES), f32),
                dma((5,)), dma((5,)), dma((5,)),
                dma((5, 2)), dma((5, 2)), dma((5, 2, 3)), dma((5, 2, 3)),
                dma((3,)), dma((3,)), dma((2,)), dma((2,)), dma((2,)),
            ],
            compiler_params=pltpu.CompilerParams(
                collective_id=0, has_side_effects=True, vmem_limit_bytes=60 << 20
            ),
        )(current_table, volt_now, volt_prev, cap_term, edge_x, edge_y, via_below, cell_ids, placed)

    spec = P("al", "gx", "gy")
    return jax.shard_map(
        block,
        mesh=mesh,
        in_specs=(spec,) * 6 + (P("gx", "gy"), P("gx", "gy"), P()),
        out_specs=(spec, spec),
        check_vma=False,
    )
```
